32 devices in a mesh: row: 2 (over core), col: 16 (over z, y, x).
Axes of the slice: x: 2, y: 2, z: 4, core: 2. Of those that a mesh axis runs over, the one named last changes fastest.
Arguments:
- tokens: bfloat16 [512, 12288], P('col', 'row'), may hold values from -6 to 6
- up_weight: bfloat16 [12288, 24576], P('row', 'col'), may hold values from -0.109375 to 0.109375
- down_weight: bfloat16 [24576, 12288], P('col', 'row'), may hold values from -0.078125 to 0.078125
- cotangent: bfloat16 [512, 12288], P('col', 'row'), may hold values from -6 to 6
- up_pattern: int32 [96, 192], P('row', 'col'), may hold values 0 or 1
- down_pattern: int32 [192, 96], P('col', 'row'), may hold values 0 or 1
Outputs:
- input_grad: bfloat16 [512, 12288], P('col', 'row')
- up_grad: bfloat16 [12288, 24576], P('row', 'col')
- down_grad: bfloat16 [24576, 12288], P('col', 'row')
The draws below stay inside these ranges and needn't reach their ends.
All inputs are finite; a program needn't handle non-finite values. No bound on the sum of `up_pattern` or of `down_pattern` on one device may be relied on, other than what follows from the above.
Results may differ from the reference program's by a relative error of at most 0.015.
Values may be sent and summed in bfloat16 or wider, within the bound.
No kernel may reach another device: no remote copies, remote signals or barrier semaphores. Data moves between devices by JAX's collectives and lax.ppermute only.
A program may use at most 192 MiB of HBM per device.

```python
import jax
import jax.numpy as jnp
from jax import lax

D = 12288
FF = 24576
BLOCK = 128
TOKENS = 512
DB = 96
FB = 192


def touch_ends(drawn, own_key, low, largest):
    spot = [jax.random.randint(jax.random.fold_in(own_key, axis), (), 0, length) for axis, length in enumerate(drawn.shape)]
    widest = drawn.shape.index(max(drawn.shape))
    next_to = spot[:widest] + [(spot[widest] + 1) % drawn.shape[widest]] + spot[widest + 1:]
    return drawn.at[tuple(spot)].set(low).at[tuple(next_to)].set(largest)


def block_scale(stream_key, extent, split, low, largest):
    loudness = 1.0
    for position, blocks in split:
        heights = jax.random.uniform(jax.random.fold_in(jax.random.fold_in(stream_key, 6), position), (blocks,), jnp.float32, low / len(split), largest / len(split))
        loudness = loudness * jnp.repeat(jnp.exp(heights), extent[position] // blocks).reshape((-1,) + (1,) * (len(extent) - 1 - position))
    return loudness


def bell_draw(key, shape, width, reach, pieces=(), held_as=jnp.bfloat16):
    values = jax.random.normal(key, shape, jnp.float32) * width
    if len(pieces) > 0:
        values = block_scale(key, shape, pieces, -0.22, 0.18) * values
    return jnp.clip(values, min=-reach, max=reach).astype(held_as)


def setup_inputs(seed: int = 0) -> dict:
    streams_of = jax.random.split(jax.random.key(seed), 7)
    tokens = bell_draw(streams_of[0], (TOKENS, D), 1.0, 6.0, ((0, 16), (1, 2)))
    up_weight = bell_draw(streams_of[1], (D, FF), (D // 4) ** -0.5, 0.109375, ((0, 2), (1, 16)))
    down_weight = bell_draw(streams_of[2], (FF, D), (FF // 4) ** -0.5, 0.078125, ((0, 16), (1, 2)))
    cotangent = bell_draw(streams_of[3], (TOKENS, D), 1.0, 6.0, ((0, 16), (1, 2)))
    up_pattern = touch_ends((jax.random.randint(streams_of[4], (DB, FB), 0, 4) < 1).astype(jnp.int32), jax.random.fold_in(streams_of[4], 1), 0, 1)
    down_pattern = touch_ends((jax.random.randint(streams_of[5], (FB, DB), 0, 4) < 1).astype(jnp.int32), jax.random.fold_in(streams_of[5], 1), 0, 1)
    return {"tokens": tokens, "up_weight": up_weight, "down_weight": down_weight, "cotangent": cotangent, "up_pattern": up_pattern, "down_pattern": down_pattern}


half_root = 0.7071067811865476
inv_root_tau = 0.3989422804014327

def widen(pattern):
    return jnp.repeat(jnp.repeat(pattern, BLOCK, axis=0), BLOCK, axis=1).astype(jnp.bfloat16)

def reference(tokens, up_weight, down_weight, cotangent, up_pattern, down_pattern):
    up_mask = widen(up_pattern)
    down_mask = widen(down_pattern)
    up_eff = up_weight * up_mask
    down_eff = down_weight * down_mask
    pre = jnp.dot(tokens, up_eff, preferred_element_type=jnp.float32)
    dact = lax.dot_general(cotangent, down_eff, (((1,), (1,)), ((), ())), preferred_element_type=jnp.float32)
    cdf = 0.5 * (1.0 + jax.scipy.special.erf(pre * half_root))
    dens = jnp.exp(-0.5 * pre * pre) * inv_root_tau
    active = (pre * cdf).astype(jnp.bfloat16)
    dhid = (dact * (cdf + pre * dens)).astype(jnp.bfloat16)
    input_grad = lax.dot_general(dhid, up_eff, (((1,), (1,)), ((), ())), preferred_element_type=jnp.float32).astype(jnp.bfloat16)
    factor = 1.0 / jnp.sqrt(jnp.float32(TOKENS))
    up_grad = lax.dot_general(tokens, dhid, (((0,), (0,)), ((), ())), preferred_element_type=jnp.float32)
    up_grad = (up_grad * up_mask.astype(jnp.float32) * factor).astype(jnp.bfloat16)
    down_grad = lax.dot_general(active, cotangent, (((0,), (0,)), ((), ())), preferred_element_type=jnp.float32)
    down_grad = (down_grad * down_mask.astype(jnp.float32) * factor).astype(jnp.bfloat16)
    return (input_grad, up_grad, down_grad)
```

```python
import functools

import jax
import jax.numpy as jnp
from jax import lax
from jax.experimental import pallas as pl
from jax.experimental.pallas import tpu as pltpu
from jax.sharding import PartitionSpec as P

half_root = 0.7071067811865476
inv_root_tau = 0.3989422804014327
GROUPS = 2
PARTS = 3
DEEP = 8
FLAT = 4


def activate(pre, dact):
    cdf = 0.5 * (1.0 + jax.scipy.special.erf(pre * half_root))
    dens = jnp.exp(-0.5 * pre * pre) * inv_root_tau
    active = (pre * cdf).astype(jnp.bfloat16)
    dhid = (dact * (cdf + pre * dens)).astype(jnp.bfloat16)
    return (active, dhid)


def stretch(count, unit):
    return -(-count // unit) * unit


def listing(pattern, unit):
    rows, columns = pattern.shape
    hit = pattern != 0
    before = jnp.arange(columns)[:, None] < jnp.arange(columns)[None, :]
    rank = jnp.sum((hit[:, :, None] & before[None]).astype(jnp.int32), axis=1)
    slots = jnp.arange(stretch(columns, unit))
    chosen = hit[:, :, None] & (rank[:, :, None] == slots[None, None, :])
    places = jnp.sum(jnp.where(chosen, jnp.arange(columns)[None, :, None], 0), axis=1)
    return (jnp.sum(hit.astype(jnp.int32), axis=1), places.reshape(-1).astype(jnp.int32))


def gated(live, block):
    return jnp.where(live, block, jnp.zeros_like(block))


def repeat(count, step):
    def body(k, carry):
        step(k)
        return carry

    lax.fori_loop(0, count, body, 0)


def runs(order, height):
    found = []
    for m in range(1 << len(order)):
        common = sum(((m >> k) & 1) << bit for k, bit in enumerate(order))
        if found and found[-1][1] + found[-1][2] == common * height:
            found[-1][2] += height
        else:
            found.append([m * height, common * height, height])
    return found


def forward_kernel(moves, block, up_n, up_at, down_n, down_at, *refs):
    arrays = 1 + max(move[0] for move in moves)
    held = refs[:arrays]
    up_hbm, down_hbm = refs[arrays : arrays + 2]
    full_ref, wide_ref, narrow_ref, up_buf, down_buf, sems, up_sem, down_sem = refs[-8:]
    columns = up_buf.shape[0]
    stride = up_buf.shape[1]

    copies = []
    for at, (array, source, target, tall, lane, breadth) in enumerate(moves):
        copies.append(
            pltpu.make_async_copy(
                held[array].at[:, pl.ds(source, tall), :],
                full_ref.at[:, pl.ds(target, tall), pl.ds(lane, breadth)],
                sems.at[at],
            )
        )
    for copy in copies:
        copy.start()

    def aligned(index):
        return pl.ds(pl.multiple_of(index * block, block), block)

    def fetch(j):
        repeat(
            up_n[j],
            lambda k: pltpu.make_async_copy(
                up_hbm.at[aligned(up_at[j * stride + k]), aligned(j)], up_buf.at[j, k], up_sem.at[j]
            ).start(),
        )
        repeat(
            down_n[j],
            lambda k: pltpu.make_async_copy(
                down_hbm.at[aligned(j), aligned(down_at[j * stride + k])],
                down_buf.at[j, k],
                down_sem.at[j],
            ).start(),
        )

    def total(which, j, count, places, buf, dim):
        def some(turn, acc):
            left, right = [], []
            for q in range(DEEP):
                k = turn * DEEP + q
                left.append(full_ref[which, :, aligned(places[j * stride + k])])
                right.append(gated(k < count, buf[j, k]))
            return acc + lax.dot_general(
                jnp.concatenate(left, 1),
                jnp.concatenate(right, dim),
                (((1,), (dim,)), ((), ())),
                preferred_element_type=jnp.float32,
            )

        start = jnp.zeros((full_ref.shape[1], block), jnp.float32)
        acc = lax.fori_loop(0, (count + DEEP - 1) // DEEP, some, start)
        wide_ref[which, :, aligned(j)] = acc
        narrow_ref[which, :, aligned(j)] = acc.astype(jnp.bfloat16)

    ahead = min(3, columns)
    for j in range(ahead):
        fetch(j)
    for copy in copies:
        copy.wait()

    def column(j):
        @pl.when(j + ahead < columns)
        def _():
            fetch(j + ahead)

        repeat(
            up_n[j],
            lambda k: pltpu.make_async_copy(
                up_hbm.at[aligned(0), aligned(0)], up_buf.at[j, k], up_sem.at[j]
            ).wait(),
        )
        total(0, j, up_n[j], up_at, up_buf, 0)
        repeat(
            down_n[j],
            lambda k: pltpu.make_async_copy(
                down_hbm.at[aligned(0), aligned(0)], down_buf.at[j, k], down_sem.at[j]
            ).wait(),
        )
        total(1, j, down_n[j], down_at, down_buf, 1)

    repeat(columns, column)


def forward(held, orders, height, up_weight, down_weight, lists, block, after):
    parts = len(held)
    width, hidden = up_weight.shape
    share = width // parts
    rows = sum(piece.shape[1] for piece in held[0])
    moves, arrays = [], []
    for part in range(parts):
        low, high = held[part]
        for source, target, tall in runs(orders[part], height):
            split = low.shape[1]
            while tall > 0:
                at = 0 if source < split else 1
                here = min(tall, split - source % split)
                moves.append(
                    (len(arrays) + at, source - at * split, target, here, part * share, share)
                )
                source, target, tall = source + here, target + here, tall - here
        arrays += [low, high]
    slots = stretch(width // block, DEEP)
    any_space = pl.BlockSpec(memory_space=pl.ANY)
    vmem = pl.BlockSpec(memory_space=pltpu.VMEM)
    smem = pl.BlockSpec(memory_space=pltpu.SMEM)
    columns = hidden // block
    return pl.pallas_call(
        functools.partial(forward_kernel, moves, block),
        in_specs=[smem] * 4 + [any_space] * (len(arrays) + 2 + len(after)),
        out_specs=[vmem] * 3,
        scratch_shapes=[
            pltpu.VMEM((columns, slots, block, block), jnp.bfloat16),
            pltpu.VMEM((columns, slots, block, block), jnp.bfloat16),
            pltpu.SemaphoreType.DMA((len(moves),)),
            pltpu.SemaphoreType.DMA((columns,)),
            pltpu.SemaphoreType.DMA((columns,)),
        ],
        out_shape=[
            jax.ShapeDtypeStruct((2, rows, width), jnp.bfloat16),
            jax.ShapeDtypeStruct((2, rows, hidden), jnp.float32),
            jax.ShapeDtypeStruct((2, rows, hidden), jnp.bfloat16),
        ],
        compiler_params=pltpu.CompilerParams(vmem_limit_bytes=56 * 1024 * 1024),
        cost_estimate=pl.CostEstimate(
            flops=4 * rows * width * hidden, bytes_accessed=width * hidden, transcendentals=0
        ),
        name="forward",
    )(*lists, *arrays, up_weight, down_weight, *after)


def backward_kernel(moves, block, first, up_n, up_at, dhid_ref, up_hbm, *refs):
    low_ref, high_ref, buf, sem = refs[-4:]
    rows, slots = buf.shape[:2]
    half = low_ref.shape[0]

    def aligned(index):
        return pl.ds(pl.multiple_of(index * block, block), block)

    def fetch(i):
        repeat(
            up_n[first + i],
            lambda k: pltpu.make_async_copy(
                up_hbm.at[aligned(first + i), aligned(up_at[(first + i) * slots + k])],
                buf.at[i, k],
                sem.at[i],
            ).start(),
        )

    repeat(rows, fetch)

    def product(i, k0):
        count = up_n[first + i]
        left, right = [], []
        for q in range(FLAT):
            left.append(dhid_ref[:, aligned(up_at[(first + i) * slots + k0 + q])])
            right.append(gated(k0 + q < count, buf[i, k0 + q]))
        return lax.dot_general(
            jnp.concatenate(left, 1),
            jnp.concatenate(right, 1),
            (((1,), (1,)), ((), ())),
            preferred_element_type=jnp.float32,
        )

    for i in range(rows):
        repeat(
            up_n[first + i],
            lambda k, i=i: pltpu.make_async_copy(
                up_hbm.at[aligned(0), aligned(0)], buf.at[i, k], sem.at[i]
            ).wait(),
        )
    together = 4 if rows % 4 == 0 else 1
    for i0 in range(0, rows, together):
        accs = [product(i0 + r, 0) for r in range(together)]
        for r in range(together):
            i = i0 + r
            turns = (up_n[first + i] + FLAT - 1) // FLAT
            acc = lax.fori_loop(
                1, turns, lambda t, acc, i=i: acc + product(i, t * FLAT), accs[r]
            ).astype(jnp.bfloat16)
            for source, target, tall in moves:
                out_ref = low_ref if source < half else high_ref
                out_ref[source % half : source % half + tall, i * block : (i + 1) * block] = acc[
                    target : target + tall
                ]


def backward(dhid, up_weight, up_n, up_at, order, height, block, part, parts, after):
    width, hidden = up_weight.shape
    rows = dhid.shape[0]
    share = width // parts
    moves = []
    for source, target, tall in runs(order, height):
        while tall > 0:
            here = min(tall, rows // 2 - source % (rows // 2))
            moves.append((source, target, here))
            source, target, tall = source + here, target + here, tall - here
    vmem = pl.BlockSpec(memory_space=pltpu.VMEM)
    smem = pl.BlockSpec(memory_space=pltpu.SMEM)
    any_space = pl.BlockSpec(memory_space=pl.ANY)
    return pl.pallas_call(
        functools.partial(backward_kernel, moves, block, part * share // block),
        in_specs=[smem, smem, vmem] + [any_space] * (1 + len(after)),
        out_specs=[vmem] * 2,
        scratch_shapes=[
            pltpu.VMEM((share // block, stretch(hidden // block, FLAT), block, block), jnp.bfloat16),
            pltpu.SemaphoreType.DMA((share // block,)),
        ],
        out_shape=[jax.ShapeDtypeStruct((rows // 2, share), jnp.bfloat16)] * 2,
        compiler_params=pltpu.CompilerParams(vmem_limit_bytes=20 * 1024 * 1024),
        cost_estimate=pl.CostEstimate(
            flops=2 * rows * share * hidden, bytes_accessed=share * hidden, transcendentals=0
        ),
        name="backward",
    )(up_n, up_at, dhid, up_weight, *after)


def grad_kernel(block, factor, first, groups, pattern, *refs):
    lefts, rights, out_ref = refs[:groups], refs[groups : 2 * groups], refs[-1]
    down, across = out_ref.shape[0] // block, out_ref.shape[1] // block
    row = first[0] + pl.program_id(0) * down
    column = first[1] + pl.program_id(1) * across
    chunk = 2 if across % 2 == 0 else 1
    left = jnp.concatenate([ref[...] for ref in lefts], axis=0)
    for c in range(0, across, chunk):
        lanes = slice(c * block, (c + chunk) * block)
        acc = lax.dot_general(
            left,
            jnp.concatenate([ref[:, lanes] for ref in rights], axis=0),
            (((0,), (0,)), ((), ())),
            preferred_element_type=jnp.float32,
        )
        for r in range(down):
            for q in range(chunk):
                scale = jnp.where(pattern[row + r, column + c + q] != 0, factor, 0.0)
                out_ref[r * block : (r + 1) * block, (c + q) * block : (c + q + 1) * block] = (
                    acc[r * block : (r + 1) * block, q * block : (q + 1) * block] * scale
                ).astype(jnp.bfloat16)


def divisor(count, most):
    return max(k for k in range(1, most + 1) if count % k == 0)


def grad(lefts, rights, pattern, block, most, left_which, right_which, shares, by_column):
    groups = len(lefts)
    tall, broad = lefts[0].shape[-1], rights[0].shape[-1]
    tile = (
        divisor(tall // block // (1 if by_column else shares), most[0]) * block,
        divisor(broad // block // (shares if by_column else 1), most[1]) * block,
    )
    rows = lefts[0].shape[-2]
    tokens = groups * rows
    factor = float(1.0 / tokens**0.5)
    steps = [tall // tile[0], broad // tile[1]]
    steps[int(by_column)] //= shares

    def spec(which, breadth, index):
        if which is None:
            return pl.BlockSpec((rows, breadth), lambda i, c, *_: (0, index(i, c)))
        return pl.BlockSpec((None, rows, breadth), lambda i, c, *_: (which, 0, index(i, c)))

    def make(share):
        off = (0, share * steps[1]) if by_column else (share * steps[0], 0)

        def call(out, after):
            in_specs = [spec(left_which, tile[0], lambda i, c: off[0] + i)] * groups
            in_specs += [spec(right_which, tile[1], lambda i, c: off[1] + c)] * groups
            args = [*lefts, *rights, *after]
            in_specs += [pl.BlockSpec(memory_space=pl.ANY)] * len(after)
            aliases = {}
            if out is not None:
                in_specs.append(pl.BlockSpec(memory_space=pl.ANY))
                args.append(out)
                aliases = {len(args): 0}
            return pl.pallas_call(
                functools.partial(
                    grad_kernel,
                    block,
                    factor,
                    (off[0] * tile[0] // block, off[1] * tile[1] // block),
                    groups,
                ),
                grid_spec=pltpu.PrefetchScalarGridSpec(
                    num_scalar_prefetch=1,
                    grid=tuple(steps),
                    in_specs=in_specs,
                    out_specs=pl.BlockSpec(tile, lambda i, c, *_: (off[0] + i, off[1] + c)),
                ),
                out_shape=jax.ShapeDtypeStruct((tall, broad), jnp.bfloat16),
                input_output_aliases=aliases,
                compiler_params=pltpu.CompilerParams(vmem_limit_bytes=32 * 1024 * 1024),
                cost_estimate=pl.CostEstimate(
                    flops=4 * tokens * tall * broad // shares,
                    bytes_accessed=2 * tall * broad // shares,
                    transcendentals=0,
                ),
                name="grad",
            )(pattern, *args)

        return call

    return [make(share) for share in range(shares)]


def add(left, right):
    return (left.astype(jnp.float32) + right.astype(jnp.float32)).astype(jnp.bfloat16)


def halves(value):
    half = value.shape[0] // 2
    return (value[:half], value[half:])


def on_device(sizes, tokens, up_weight, down_weight, cotangent, up_pattern, down_pattern):
    n, across = sizes["col"], sizes["row"]
    bits = n.bit_length() - 1
    far = list(range(bits - 1, 1, -1))
    outer, near = far[:-1], far[-1:]
    orders = [[*outer, 1, *near, 0], [*outer, *near, 0, 1], [*outer, 0, 1, *near]]
    width, hidden = up_weight.shape
    block = width // up_pattern.shape[0]
    share = width // PARTS
    height = tokens.shape[0] // GROUPS

    def swap(value, bit):
        return lax.ppermute(value, "col", [(i, i ^ (1 << bit)) for i in range(n)])

    def beside(wide, narrow):
        for bit in range(across.bit_length() - 1):
            other = lax.ppermute(
                narrow, "row", [(i, i ^ (1 << bit)) for i in range(across)]
            )
            wide = wide + other.astype(jnp.float32)
            narrow = wide.astype(jnp.bfloat16)
        return wide

    up_n, up_at = listing(up_pattern.T, DEEP)
    down_n, down_at = listing(down_pattern, DEEP)
    back_n, back_at = listing(up_pattern, FLAT)

    helds = []
    for g in range(GROUPS):
        rows = slice(g * height, (g + 1) * height)
        own = jnp.stack([tokens[rows], cotangent[rows]])
        for bit in outer:
            own = jnp.concatenate([own, swap(own, bit)], axis=1)
        held = []
        for part in range(PARTS):
            low = own[:, :, part * share : (part + 1) * share]
            rest = orders[part][len(outer) :]
            for bit in rest[:-1]:
                low = jnp.concatenate([low, swap(low, bit)], axis=1)
            held.append((low, swap(low, rest[-1])))
        helds.append(held)

    fulls, actives, dhids, totals = [], [], [], []
    for g in range(GROUPS):
        after = [low for low, high in helds[g + 1]] if g + 1 < GROUPS else []
        full, wide, narrow = forward(
            helds[g], orders, height, up_weight, down_weight, (up_n, up_at, down_n, down_at), block, after
        )
        whole = beside(wide, narrow)
        active, dhid = activate(whole[0], whole[1])
        fulls.append(full)
        actives.append(active)
        dhids.append(dhid)
        totals.append(
            [
                backward(dhid, up_weight, back_n, back_at, orders[part], height, block, part, PARTS, [])
                for part in range(PARTS)
            ]
        )

    grads = [
        grad(fulls, dhids, up_pattern, block, (8, 12), 0, None, 3, False),
        grad(actives, fulls, down_pattern, block, (12, 8), None, 1, 3, True),
    ]
    work = [(which, call) for pair in zip(*grads) for which, call in enumerate(pair)]
    outs = [None, None]

    def advance(count, after):
        for which, call in work[:count]:
            outs[which] = call(outs[which], after)
        del work[:count]

    shares = []
    for g in range(GROUPS):
        last = g == GROUPS - 1
        held = totals[g]
        if last:
            advance(2, [half for pair in held for half in pair])
        stages = len(orders[0]) - len(outer)
        for stage in range(stages):
            summed = [
                add(low, swap(high, orders[part][-1 - stage]))
                for part, (low, high) in enumerate(held)
            ]
            if stage < stages - 1:
                held = [halves(total) for total in summed]
                if last:
                    advance(2 if stage == 0 else 1, summed)
        total = jnp.concatenate(summed, axis=1)
        if last:
            advance(1, [total])
        for bit in reversed(outer):
            low, high = halves(total)
            total = add(low, swap(high, bit))
        shares.append(total)
    input_grad = jnp.concatenate(shares, axis=0)
    advance(len(work), [])
    return (input_grad, outs[0], outs[1])


def solution(mesh):
    return jax.shard_map(
        functools.partial(on_device, dict(mesh.shape)),
        mesh=mesh,
        in_specs=(
            P("col", "row"),
            P("row", "col"),
            P("col", "row"),
            P("col", "row"),
            P("row", "col"),
            P("col", "row"),
        ),
        out_specs=(P("col", "row"), P("row", "col"), P("col", "row")),
        check_vma=False,
    )
```

```python
import functools

import jax
import jax.numpy as jnp
from jax import lax
from jax.experimental import pallas as pl
from jax.experimental.pallas import tpu as pltpu
from jax.sharding import PartitionSpec as P

half_root = 0.7071067811865476
inv_root_tau = 0.3989422804014327
GROUPS = 2
SPLIT = (18, 20)
OUT_OF = 48


def activate(pre, dact):
    cdf = 0.5 * (1.0 + jax.scipy.special.erf(pre * half_root))
    dens = jnp.exp(-0.5 * pre * pre) * inv_root_tau
    active = (pre * cdf).astype(jnp.bfloat16)
    dhid = (dact * (cdf + pre * dens)).astype(jnp.bfloat16)
    return (active, dhid)


def divisor(count, most):
    return max(k for k in range(1, most + 1) if count % k == 0)


def kept(flag, block):
    return jnp.where(flag != 0, block, jnp.zeros_like(block))


def runs(order, height, half):
    found = []
    for m in range(1 << len(order)):
        common = sum(((m >> k) & 1) << bit for k, bit in enumerate(order)) * height
        side, row = divmod(m * height, half)
        last = found[-1] if found else None
        if last and last[0] == side and last[2] + last[3] == common:
            last[3] += height
        else:
            found.append([side, row, common, height])
    return found


def forward_kernel(moves, block, up_on, down_on, *refs):
    arrays = 1 + max(move[0] for move in moves)
    held = refs[:arrays]
    up_hbm, down_hbm = refs[arrays : arrays + 2]
    full_hbm, *sum_hbm = refs[-11:-8]
    full, sums, up_buf, down_buf = refs[-8:-4]
    in_sems, out_sems, weight_sems, full_sem = refs[-4:]
    rows, width = full.shape[1:]
    columns, down = sums.shape[2] // block, width // block
    slots, each = up_buf.shape[0], up_buf.shape[2] // block
    turns = columns // each

    def here(turn):
        return pl.ds(pl.multiple_of(turn * each * block, each * block), each * block)

    def fetch(turn):
        slot = lax.rem(turn, slots)
        return (
            pltpu.make_async_copy(up_hbm.at[:, here(turn)], up_buf.at[slot], weight_sems.at[0, slot]),
            pltpu.make_async_copy(down_hbm.at[here(turn), :], down_buf.at[slot], weight_sems.at[1, slot]),
        )

    copies = [
        pltpu.make_async_copy(
            held[array].at[:, pl.ds(source, tall), :],
            full.at[:, pl.ds(target, tall), pl.ds(lane, breadth)],
            in_sems.at[at],
        )
        for at, (array, source, target, tall, lane, breadth) in enumerate(moves)
    ]
    for copy in copies:
        copy.start()
    for turn in range(min(slots, turns)):
        for copy in fetch(turn):
            copy.start()
    for copy in copies:
        copy.wait()
    whole = pltpu.make_async_copy(full, full_hbm, full_sem)
    whole.start()

    def leave(turn):
        return [
            pltpu.make_async_copy(
                sums.at[w, :, here(turn)], sum_hbm[w].at[:, here(turn)], out_sems.at[w, turn]
            )
            for w in range(2)
        ]

    def step(turn, carry):
        lanes = here(turn)
        slot = lax.rem(turn, slots)
        for copy in fetch(turn):
            copy.wait()
        right = jnp.concatenate(
            [
                jnp.concatenate(
                    [
                        kept(
                            up_on[i, turn * each + c],
                            up_buf[slot, i * block : (i + 1) * block, c * block : (c + 1) * block],
                        )
                        for c in range(each)
                    ],
                    1,
                )
                for i in range(down)
            ],
            0,
        )
        pre = jnp.dot(full[0], right, preferred_element_type=jnp.float32)
        sums[0, :, lanes] = pre.astype(jnp.bfloat16)
        right = jnp.concatenate(
            [
                jnp.concatenate(
                    [
                        kept(
                            down_on[turn * each + c, i],
                            down_buf[
                                slot, c * block : (c + 1) * block, i * block : (i + 1) * block
                            ],
                        )
                        for i in range(down)
                    ],
                    1,
                )
                for c in range(each)
            ],
            0,
        )
        dact = lax.dot_general(
            full[1], right, (((1,), (1,)), ((), ())), preferred_element_type=jnp.float32
        )
        sums[1, :, lanes] = dact.astype(jnp.bfloat16)

        @pl.when(turn + slots < turns)
        def _():
            for copy in fetch(turn + slots):
                copy.start()

        for copy in leave(turn):
            copy.start()
        return carry

    lax.fori_loop(0, turns, step, 0)
    for turn in range(turns):
        for copy in leave(turn):
            copy.wait()
    whole.wait()


def forward(held, orders, height, up_weight, down_weight, up_on, down_on, after):
    width, hidden = up_weight.shape
    block = width // up_on.shape[0]
    rows = 2 * held[0][0].shape[1]
    moves, arrays, lane = [], [], 0
    for (low, high), order in zip(held, orders):
        for side, source, target, tall in runs(order, height, rows // 2):
            moves.append((len(arrays) + side, source, target, tall, lane, low.shape[2]))
        arrays += [low, high]
        lane += low.shape[2]
    any_space = pl.BlockSpec(memory_space=pl.ANY)
    smem = pl.BlockSpec(memory_space=pltpu.SMEM)
    each = divisor(hidden // block, 2)
    slots = 3
    shapes = [
        ((2, rows, width), jnp.bfloat16),
        ((2, rows, hidden), jnp.bfloat16),
    ]
    return pl.pallas_call(
        functools.partial(forward_kernel, moves, block),
        in_specs=[smem] * 2 + [any_space] * (len(arrays) + 2 + len(after)),
        out_specs=[any_space] * 3,
        scratch_shapes=[pltpu.VMEM(*shape) for shape in shapes]
        + [
            pltpu.VMEM((slots, width, each * block), jnp.bfloat16),
            pltpu.VMEM((slots, each * block, width), jnp.bfloat16),
            pltpu.SemaphoreType.DMA((len(moves),)),
            pltpu.SemaphoreType.DMA((2, hidden // block // each)),
            pltpu.SemaphoreType.DMA((2, slots)),
            pltpu.SemaphoreType.DMA,
        ],
        out_shape=[jax.ShapeDtypeStruct(*shape) for shape in shapes[:1]]
        + [jax.ShapeDtypeStruct((rows, hidden), jnp.bfloat16)] * 2,
        compiler_params=pltpu.CompilerParams(vmem_limit_bytes=48 * 1024 * 1024),
        cost_estimate=pl.CostEstimate(
            flops=rows * width, bytes_accessed=rows * width, transcendentals=0
        ),
        name="forward",
    )(up_on, down_on, *arrays, up_weight, down_weight, *after)


def backward_kernel(parts, block, up_on, dhid_ref, up_hbm, *refs):
    outs, (buf, sems) = refs[-2 - 2 * len(parts) : -2], refs[-2:]
    across = up_hbm.shape[1] // block
    tiles, at = [], 0
    for part, (moves, count) in enumerate(parts):
        each = divisor(count, 6)
        tiles += [(part, moves, at + r, r, each) for r in range(0, count, each)]
        at += count
    copies = []
    for k, (part, moves, row, lane, each) in enumerate(tiles):
        rows = pl.ds(row * block, each * block)
        copies.append(pltpu.make_async_copy(up_hbm.at[rows, :], buf.at[rows, :], sems.at[k]))
    for copy in copies:
        copy.start()
    for copy, (part, moves, row, lane, each) in zip(copies, tiles):
        copy.wait()
        right = jnp.concatenate(
            [
                jnp.concatenate(
                    [
                        kept(
                            up_on[row + r, c],
                            buf[(row + r) * block : (row + r + 1) * block, c * block : (c + 1) * block],
                        )
                        for c in range(across)
                    ],
                    1,
                )
                for r in range(each)
            ],
            0,
        )
        acc = lax.dot_general(
            dhid_ref[...], right, (((1,), (1,)), ((), ())), preferred_element_type=jnp.float32
        ).astype(jnp.bfloat16)
        for side, target, source, tall in moves:
            outs[2 * part + side][
                target : target + tall, lane * block : (lane + each) * block
            ] = acc[source : source + tall]


def backward(dhid, up_weight, up_on, orders, height, bounds, after):
    width, hidden = up_weight.shape
    block = width // up_on.shape[0]
    rows = dhid.shape[0]
    parts = [
        (runs(order, height, rows // 2), (stop - start) // block)
        for order, (start, stop) in zip(orders, bounds)
    ]
    tiles = sum(count // divisor(count, 6) for moves, count in parts)
    vmem = pl.BlockSpec(memory_space=pltpu.VMEM)
    smem = pl.BlockSpec(memory_space=pltpu.SMEM)
    any_space = pl.BlockSpec(memory_space=pl.ANY)
    outs = pl.pallas_call(
        functools.partial(backward_kernel, parts, block),
        in_specs=[smem, vmem] + [any_space] * (1 + len(after)),
        out_specs=[vmem] * (2 * len(parts)),
        scratch_shapes=[pltpu.VMEM((width, hidden), jnp.bfloat16), pltpu.SemaphoreType.DMA((tiles,))],
        out_shape=[
            jax.ShapeDtypeStruct((rows // 2, count * block), jnp.bfloat16)
            for moves, count in parts
            for side in range(2)
        ],
        compiler_params=pltpu.CompilerParams(vmem_limit_bytes=48 * 1024 * 1024),
        cost_estimate=pl.CostEstimate(
            flops=rows * width, bytes_accessed=rows * width, transcendentals=0
        ),
        name="backward",
    )(up_on, dhid, up_weight, *after)
    return [(outs[2 * part], outs[2 * part + 1]) for part in range(len(parts))]


def grad_kernel(block, factor, first, groups, pattern, *refs):
    lefts, rights, out_ref = refs[:groups], refs[groups : 2 * groups], refs[-1]
    down, across = out_ref.shape[0] // block, out_ref.shape[1] // block
    row = first[0] + pl.program_id(0) * down
    column = first[1] + pl.program_id(1) * across
    chunk = 2 if across % 2 == 0 else 1
    left = jnp.concatenate([ref[...] for ref in lefts], axis=0)
    for c in range(0, across, chunk):
        lanes = slice(c * block, (c + chunk) * block)
        acc = lax.dot_general(
            left,
            jnp.concatenate([ref[:, lanes] for ref in rights], axis=0),
            (((0,), (0,)), ((), ())),
            preferred_element_type=jnp.float32,
        )
        for r in range(down):
            for q in range(chunk):
                scale = jnp.where(pattern[row + r, column + c + q] != 0, factor, 0.0)
                out_ref[r * block : (r + 1) * block, (c + q) * block : (c + q + 1) * block] = (
                    acc[r * block : (r + 1) * block, q * block : (q + 1) * block] * scale
                ).astype(jnp.bfloat16)


def grad(lefts, rights, pattern, block, most, left_which, right_which, shares, by_column):
    groups = len(lefts)
    tall, broad = lefts[0].shape[-1], rights[0].shape[-1]
    tile = (
        divisor(tall // block // (1 if by_column else shares), most[0]) * block,
        divisor(broad // block // (shares if by_column else 1), most[1]) * block,
    )
    rows = lefts[0].shape[-2]
    tokens = groups * rows
    factor = float(1.0 / tokens**0.5)
    steps = [tall // tile[0], broad // tile[1]]
    steps[int(by_column)] //= shares

    def spec(which, breadth, index):
        if which is None:
            return pl.BlockSpec((rows, breadth), lambda i, c, *_: (0, index(i, c)))
        return pl.BlockSpec((None, rows, breadth), lambda i, c, *_: (which, 0, index(i, c)))

    def make(share):
        off = (0, share * steps[1]) if by_column else (share * steps[0], 0)

        def call(out, after):
            in_specs = [spec(left_which, tile[0], lambda i, c: off[0] + i)] * groups
            in_specs += [spec(right_which, tile[1], lambda i, c: off[1] + c)] * groups
            args = [*lefts, *rights, *after]
            in_specs += [pl.BlockSpec(memory_space=pl.ANY)] * len(after)
            aliases = {}
            if out is not None:
                in_specs.append(pl.BlockSpec(memory_space=pl.ANY))
                args.append(out)
                aliases = {len(args): 0}
            return pl.pallas_call(
                functools.partial(
                    grad_kernel,
                    block,
                    factor,
                    (off[0] * tile[0] // block, off[1] * tile[1] // block),
                    groups,
                ),
                grid_spec=pltpu.PrefetchScalarGridSpec(
                    num_scalar_prefetch=1,
                    grid=tuple(steps),
                    in_specs=in_specs,
                    out_specs=pl.BlockSpec(tile, lambda i, c, *_: (off[0] + i, off[1] + c)),
                ),
                out_shape=jax.ShapeDtypeStruct((tall, broad), jnp.bfloat16),
                input_output_aliases=aliases,
                compiler_params=pltpu.CompilerParams(vmem_limit_bytes=32 * 1024 * 1024),
                cost_estimate=pl.CostEstimate(
                    flops=2 * tokens * tall * broad // shares,
                    bytes_accessed=2 * tall * broad // shares,
                    transcendentals=0,
                ),
                name="grad",
            )(pattern, *args)

        return call

    return [make(share) for share in range(shares)]


def add(left, right):
    return (left.astype(jnp.float32) + right.astype(jnp.float32)).astype(jnp.bfloat16)


def halves(value):
    half = value.shape[0] // 2
    return (value[:half], value[half:])


def on_device(sizes, tokens, up_weight, down_weight, cotangent, up_pattern, down_pattern):
    n, across = sizes["col"], sizes["row"]
    bits = n.bit_length() - 1
    far = list(range(bits - 1, 1, -1))
    outer, near = far[:-1], far[-1:]
    orders = [[*outer, 1, *near, 0], [*outer, *near, 0, 1], [*outer, 0, 1, *near]]
    width, hidden = up_weight.shape
    down = up_pattern.shape[0]
    block = width // down
    height = tokens.shape[0] // GROUPS
    bounds = [0, SPLIT[0] * down // OUT_OF, sum(SPLIT) * down // OUT_OF, down]
    bounds = [(at * block, to * block) for at, to in zip(bounds, bounds[1:])]

    def swap(value, bit):
        return lax.ppermute(value, "col", [(i, i ^ (1 << bit)) for i in range(n)])

    def later(value, *marks):
        return lax.optimization_barrier((value, *marks))[0]

    def beside(sums, marks):
        for bit in range(across.bit_length() - 1):
            pairs = [(i, i ^ (1 << bit)) for i in range(across)]
            others = [later(lax.ppermute(part.astype(jnp.bfloat16), "row", pairs), *marks) for part in sums]
            sums = [
                part.astype(jnp.float32) + other.astype(jnp.float32) for part, other in zip(sums, others)
            ]
        return sums

    helds = []
    for g in range(GROUPS):
        rows = slice(g * height, (g + 1) * height)
        own = jnp.stack([tokens[rows], cotangent[rows]])
        if g > 0:
            own = later(own, *ahead)
        for bit in outer:
            own = jnp.concatenate([own, swap(own, bit)], axis=1)
        if g > 0:
            own = later(own, *helds[-1])
        held, ahead = [], []
        for part, (start, stop) in enumerate(bounds):
            low = own[:, :, start:stop]
            rest = orders[part][len(outer) :]
            for bit in rest[:-1]:
                low = jnp.concatenate([low, swap(low, bit)], axis=1)
                if bit == rest[0]:
                    ahead.append(low)
            held.append(low)
        helds.append(held)
    for g, held in enumerate(helds):
        marks = helds[g + 1] if g + 1 < GROUPS else []
        helds[g] = [(low, swap(later(low, *marks), order[-1])) for low, order in zip(held, orders)]

    def stage(held, at, mark, marked):
        summed = []
        for part, (low, high) in enumerate(held):
            other = swap(high, orders[part][-1 - at])
            summed.append(add(low, other if mark is None or part >= marked else later(other, mark)))
        return summed

    def finish(summed, mark):
        total = jnp.concatenate(summed, axis=1)
        for bit in reversed(outer):
            low, high = halves(total)
            other = swap(high, bit)
            total = add(low, other if mark is None else later(other, mark))
        return total

    stages = len(orders[0]) - len(outer)
    last = GROUPS - 1
    fulls, actives, dhids, totals = [], [], [], []
    for g in range(GROUPS):
        after = [low for low, high in helds[g + 1]] if g + 1 < GROUPS else []
        after = after + ([half for pair in totals[-1] for half in pair] if g > 0 else [])
        full, *sums = forward(
            helds[g], orders, height, up_weight, down_weight, up_pattern, down_pattern, after
        )
        marks = [high for low, high in helds[g + 1][:2]] if g + 1 < GROUPS else []
        active, dhid = activate(*beside(sums, marks))
        fulls.append(full)
        actives.append(active)
        dhids.append(dhid)
        early, after = totals, []
        if g == last:
            for at, mark in zip(range(stages - 1), (sums[1], dhid)):
                early = [stage(held, at, mark, len(orders)) for held in early]
                after = [total for summed in early for total in summed]
                early = [[halves(total) for total in summed] for summed in early]
        totals.append(
            backward(dhid, up_weight, up_pattern, orders, height, bounds, after)
        )

    grads = [
        grad(fulls, dhids, up_pattern, block, (8, 12), 0, None, 2, False),
        grad(actives, fulls, down_pattern, block, (12, 8), None, 1, 2, True),
    ]
    work = [(which, call) for pair in zip(*grads) for which, call in enumerate(pair)]
    outs = [None, None]

    def advance(count, after):
        for which, call in work[:count]:
            outs[which] = call(outs[which], after)
        del work[:count]

    held = totals[last]
    late = [stage(pairs, stages - 1, held[0][0], len(orders)) for pairs in early]
    advance(2, [half for pair in held for half in pair] + [total for summed in late for total in summed])
    shares = [finish(summed, outs[1]) for summed in late]
    for at in range(stages):
        summed = stage(held, at, outs[1 - at] if at < 2 else None, 2)
        if at == 0:
            advance(1, summed)
        if at < stages - 1:
            summed = lax.optimization_barrier(summed)
        held = [halves(total) for total in summed]
    advance(len(work), summed)
    shares.append(finish(summed, None))
    input_grad = jnp.concatenate(shares, axis=0)
    return (input_grad, outs[0], outs[1])


def solution(mesh):
    return jax.shard_map(
        functools.partial(on_device, dict(mesh.shape)),
        mesh=mesh,
        in_specs=(
            P("col", "row"),
            P("row", "col"),
            P("col", "row"),
            P("col", "row"),
            P("row", "col"),
            P("col", "row"),
        ),
        out_specs=(P("col", "row"), P("row", "col"), P("col", "row")),
        check_vma=False,
    )
```

```python
import functools

import jax
import jax.numpy as jnp
from jax import lax
from jax.experimental import pallas as pl
from jax.experimental.pallas import tpu as pltpu
from jax.sharding import PartitionSpec as P

half_root = 0.7071067811865476
inv_root_tau = 0.3989422804014327
GROUPS = 2
SPLIT = (18, 20)
OUT_OF = 48


def activate(pre, dact):
    cdf = 0.5 * (1.0 + jax.scipy.special.erf(pre * half_root))
    dens = jnp.exp(-0.5 * pre * pre) * inv_root_tau
    active = (pre * cdf).astype(jnp.bfloat16)
    dhid = (dact * (cdf + pre * dens)).astype(jnp.bfloat16)
    return (active, dhid)


def divisor(count, most):
    return max(k for k in range(1, most + 1) if count % k == 0)


def kept(flag, block):
    return jnp.where(flag != 0, block, jnp.zeros_like(block))


def runs(order, height, half):
    found = []
    for m in range(1 << len(order)):
        common = sum(((m >> k) & 1) << bit for k, bit in enumerate(order)) * height
        side, row = divmod(m * height, half)
        last = found[-1] if found else None
        if last and last[0] == side and last[2] + last[3] == common:
            last[3] += height
        else:
            found.append([side, row, common, height])
    return found


def forward_kernel(moves, block, up_on, down_on, *refs):
    arrays = 1 + max(move[0] for move in moves)
    held = refs[:arrays]
    up_hbm, down_hbm = refs[arrays : arrays + 2]
    full_hbm, *sum_hbm = refs[-11:-8]
    full, sums, up_buf, down_buf = refs[-8:-4]
    in_sems, out_sems, weight_sems, full_sem = refs[-4:]
    rows, width = full.shape[1:]
    columns, down = sums.shape[2] // block, width // block
    slots, each = up_buf.shape[0], up_buf.shape[2] // block
    turns = columns // each

    def here(turn):
        return pl.ds(pl.multiple_of(turn * each * block, each * block), each * block)

    def fetch(turn):
        slot = lax.rem(turn, slots)
        return (
            pltpu.make_async_copy(up_hbm.at[:, here(turn)], up_buf.at[slot], weight_sems.at[0, slot]),
            pltpu.make_async_copy(down_hbm.at[here(turn), :], down_buf.at[slot], weight_sems.at[1, slot]),
        )

    copies = [
        pltpu.make_async_copy(
            held[array].at[:, pl.ds(source, tall), :],
            full.at[:, pl.ds(target, tall), pl.ds(lane, breadth)],
            in_sems.at[at],
        )
        for at, (array, source, target, tall, lane, breadth) in enumerate(moves)
    ]
    for copy in copies:
        copy.start()
    for turn in range(min(slots, turns)):
        for copy in fetch(turn):
            copy.start()
    for copy in copies:
        copy.wait()
    whole = pltpu.make_async_copy(full, full_hbm, full_sem)
    whole.start()

    def leave(turn):
        return [
            pltpu.make_async_copy(
                sums.at[w, :, here(turn)], sum_hbm[w].at[:, here(turn)], out_sems.at[w, turn]
            )
            for w in range(2)
        ]

    def step(turn, carry):
        lanes = here(turn)
        slot = lax.rem(turn, slots)
        for copy in fetch(turn):
            copy.wait()
        right = jnp.concatenate(
            [
                jnp.concatenate(
                    [
                        kept(
                            up_on[i, turn * each + c],
                            up_buf[slot, i * block : (i + 1) * block, c * block : (c + 1) * block],
                        )
                        for c in range(each)
                    ],
                    1,
                )
                for i in range(down)
            ],
            0,
        )
        pre = jnp.dot(full[0], right, preferred_element_type=jnp.float32)
        sums[0, :, lanes] = pre.astype(jnp.bfloat16)
        right = jnp.concatenate(
            [
                jnp.concatenate(
                    [
                        kept(
                            down_on[turn * each + c, i],
                            down_buf[
                                slot, c * block : (c + 1) * block, i * block : (i + 1) * block
                            ],
                        )
                        for i in range(down)
                    ],
                    1,
                )
                for c in range(each)
            ],
            0,
        )
        dact = lax.dot_general(
            full[1], right, (((1,), (1,)), ((), ())), preferred_element_type=jnp.float32
        )
        sums[1, :, lanes] = dact.astype(jnp.bfloat16)

        @pl.when(turn + slots < turns)
        def _():
            for copy in fetch(turn + slots):
                copy.start()

        for copy in leave(turn):
            copy.start()
        return carry

    lax.fori_loop(0, turns, step, 0)
    for turn in range(turns):
        for copy in leave(turn):
            copy.wait()
    whole.wait()


def forward(held, orders, height, up_weight, down_weight, up_on, down_on, after):
    width, hidden = up_weight.shape
    block = width // up_on.shape[0]
    rows = 2 * held[0][0].shape[1]
    moves, arrays, lane = [], [], 0
    for (low, high), order in zip(held, orders):
        for side, source, target, tall in runs(order, height, rows // 2):
            moves.append((len(arrays) + side, source, target, tall, lane, low.shape[2]))
        arrays += [low, high]
        lane += low.shape[2]
    any_space = pl.BlockSpec(memory_space=pl.ANY)
    smem = pl.BlockSpec(memory_space=pltpu.SMEM)
    each = divisor(hidden // block, 2)
    slots = 3
    shapes = [
        ((2, rows, width), jnp.bfloat16),
        ((2, rows, hidden), jnp.bfloat16),
    ]
    return pl.pallas_call(
        functools.partial(forward_kernel, moves, block),
        in_specs=[smem] * 2 + [any_space] * (len(arrays) + 2 + len(after)),
        out_specs=[any_space] * 3,
        scratch_shapes=[pltpu.VMEM(*shape) for shape in shapes]
        + [
            pltpu.VMEM((slots, width, each * block), jnp.bfloat16),
            pltpu.VMEM((slots, each * block, width), jnp.bfloat16),
            pltpu.SemaphoreType.DMA((len(moves),)),
            pltpu.SemaphoreType.DMA((2, hidden // block // each)),
            pltpu.SemaphoreType.DMA((2, slots)),
            pltpu.SemaphoreType.DMA,
        ],
        out_shape=[jax.ShapeDtypeStruct(*shape) for shape in shapes[:1]]
        + [jax.ShapeDtypeStruct((rows, hidden), jnp.bfloat16)] * 2,
        compiler_params=pltpu.CompilerParams(vmem_limit_bytes=48 * 1024 * 1024),
        cost_estimate=pl.CostEstimate(
            flops=rows * width, bytes_accessed=rows * width, transcendentals=0
        ),
        name="forward",
    )(up_on, down_on, *arrays, up_weight, down_weight, *after)


def backward_kernel(parts, block, up_on, dhid_ref, up_hbm, *refs):
    outs, (buf, sems) = refs[-2 - 2 * len(parts) : -2], refs[-2:]
    across = up_hbm.shape[1] // block
    tiles, at = [], 0
    for part, (moves, count) in enumerate(parts):
        each = divisor(count, 6)
        tiles += [(part, moves, at + r, r, each) for r in range(0, count, each)]
        at += count
    copies = []
    for k, (part, moves, row, lane, each) in enumerate(tiles):
        rows = pl.ds(row * block, each * block)
        copies.append(pltpu.make_async_copy(up_hbm.at[rows, :], buf.at[rows, :], sems.at[k]))
    for copy in copies:
        copy.start()
    for copy, (part, moves, row, lane, each) in zip(copies, tiles):
        copy.wait()
        right = jnp.concatenate(
            [
                jnp.concatenate(
                    [
                        kept(
                            up_on[row + r, c],
                            buf[(row + r) * block : (row + r + 1) * block, c * block : (c + 1) * block],
                        )
                        for c in range(across)
                    ],
                    1,
                )
                for r in range(each)
            ],
            0,
        )
        acc = lax.dot_general(
            dhid_ref[...], right, (((1,), (1,)), ((), ())), preferred_element_type=jnp.float32
        ).astype(jnp.bfloat16)
        for side, target, source, tall in moves:
            outs[2 * part + side][
                target : target + tall, lane * block : (lane + each) * block
            ] = acc[source : source + tall]


def backward(dhid, up_weight, up_on, orders, height, bounds, after):
    width, hidden = up_weight.shape
    block = width // up_on.shape[0]
    rows = dhid.shape[0]
    parts = [
        (runs(order, height, rows // 2), (stop - start) // block)
        for order, (start, stop) in zip(orders, bounds)
    ]
    tiles = sum(count // divisor(count, 6) for moves, count in parts)
    vmem = pl.BlockSpec(memory_space=pltpu.VMEM)
    smem = pl.BlockSpec(memory_space=pltpu.SMEM)
    any_space = pl.BlockSpec(memory_space=pl.ANY)
    outs = pl.pallas_call(
        functools.partial(backward_kernel, parts, block),
        in_specs=[smem, vmem] + [any_space] * (1 + len(after)),
        out_specs=[vmem] * (2 * len(parts)),
        scratch_shapes=[pltpu.VMEM((width, hidden), jnp.bfloat16), pltpu.SemaphoreType.DMA((tiles,))],
        out_shape=[
            jax.ShapeDtypeStruct((rows // 2, count * block), jnp.bfloat16)
            for moves, count in parts
            for side in range(2)
        ],
        compiler_params=pltpu.CompilerParams(vmem_limit_bytes=48 * 1024 * 1024),
        cost_estimate=pl.CostEstimate(
            flops=rows * width, bytes_accessed=rows * width, transcendentals=0
        ),
        name="backward",
    )(up_on, dhid, up_weight, *after)
    return [(outs[2 * part], outs[2 * part + 1]) for part in range(len(parts))]


def grad_kernel(block, factor, first, groups, pattern, *refs):
    lefts, rights, out_ref = refs[:groups], refs[groups : 2 * groups], refs[-1]
    down, across = out_ref.shape[0] // block, out_ref.shape[1] // block
    row = first[0] + pl.program_id(0) * down
    column = first[1] + pl.program_id(1) * across
    chunk = 2 if across % 2 == 0 else 1
    left = jnp.concatenate([ref[...] for ref in lefts], axis=0)
    for c in range(0, across, chunk):
        lanes = slice(c * block, (c + chunk) * block)
        acc = lax.dot_general(
            left,
            jnp.concatenate([ref[:, lanes] for ref in rights], axis=0),
            (((0,), (0,)), ((), ())),
            preferred_element_type=jnp.float32,
        )
        for r in range(down):
            for q in range(chunk):
                scale = jnp.where(pattern[row + r, column + c + q] != 0, factor, 0.0)
                out_ref[r * block : (r + 1) * block, (c + q) * block : (c + q + 1) * block] = (
                    acc[r * block : (r + 1) * block, q * block : (q + 1) * block] * scale
                ).astype(jnp.bfloat16)


def grad(lefts, rights, pattern, block, most, left_which, right_which, shares, by_column):
    groups = len(lefts)
    tall, broad = lefts[0].shape[-1], rights[0].shape[-1]
    tile = (
        divisor(tall // block // (1 if by_column else shares), most[0]) * block,
        divisor(broad // block // (shares if by_column else 1), most[1]) * block,
    )
    rows = lefts[0].shape[-2]
    tokens = groups * rows
    factor = float(1.0 / tokens**0.5)
    steps = [tall // tile[0], broad // tile[1]]
    steps[int(by_column)] //= shares

    def spec(which, breadth, index):
        if which is None:
            return pl.BlockSpec((rows, breadth), lambda i, c, *_: (0, index(i, c)))
        return pl.BlockSpec((None, rows, breadth), lambda i, c, *_: (which, 0, index(i, c)))

    def make(share):
        off = (0, share * steps[1]) if by_column else (share * steps[0], 0)

        def call(out, after):
            in_specs = [spec(left_which, tile[0], lambda i, c: off[0] + i)] * groups
            in_specs += [spec(right_which, tile[1], lambda i, c: off[1] + c)] * groups
            args = [*lefts, *rights, *after]
            in_specs += [pl.BlockSpec(memory_space=pl.ANY)] * len(after)
            aliases = {}
            if out is not None:
                in_specs.append(pl.BlockSpec(memory_space=pl.ANY))
                args.append(out)
                aliases = {len(args): 0}
            return pl.pallas_call(
                functools.partial(
                    grad_kernel,
                    block,
                    factor,
                    (off[0] * tile[0] // block, off[1] * tile[1] // block),
                    groups,
                ),
                grid_spec=pltpu.PrefetchScalarGridSpec(
                    num_scalar_prefetch=1,
                    grid=tuple(steps),
                    in_specs=in_specs,
                    out_specs=pl.BlockSpec(tile, lambda i, c, *_: (off[0] + i, off[1] + c)),
                ),
                out_shape=jax.ShapeDtypeStruct((tall, broad), jnp.bfloat16),
                input_output_aliases=aliases,
                compiler_params=pltpu.CompilerParams(vmem_limit_bytes=32 * 1024 * 1024),
                cost_estimate=pl.CostEstimate(
                    flops=tall * broad // shares,
                    bytes_accessed=tokens * broad // shares,
                    transcendentals=0,
                ),
                name="grad",
            )(pattern, *args)

        return call

    return [make(share) for share in range(shares)]


def add(left, right):
    return (left.astype(jnp.float32) + right.astype(jnp.float32)).astype(jnp.bfloat16)


def halves(value):
    half = value.shape[0] // 2
    return (value[:half], value[half:])


def on_device(sizes, tokens, up_weight, down_weight, cotangent, up_pattern, down_pattern):
    n, across = sizes["col"], sizes["row"]
    bits = n.bit_length() - 1
    far = list(range(bits - 1, 1, -1))
    outer, near = far[:-1], far[-1:]
    orders = [[*outer, 1, *near, 0], [*outer, *near, 0, 1], [*outer, 0, 1, *near]]
    width, hidden = up_weight.shape
    down = up_pattern.shape[0]
    block = width // down
    height = tokens.shape[0] // GROUPS
    bounds = [0, SPLIT[0] * down // OUT_OF, sum(SPLIT) * down // OUT_OF, down]
    bounds = [(at * block, to * block) for at, to in zip(bounds, bounds[1:])]

    def swap(value, bit):
        return lax.ppermute(value, "col", [(i, i ^ (1 << bit)) for i in range(n)])

    def later(value, *marks):
        return lax.optimization_barrier((value, *marks))[0]

    def beside(sums, marks):
        for bit in range(across.bit_length() - 1):
            pairs = [(i, i ^ (1 << bit)) for i in range(across)]
            others = [later(lax.ppermute(part.astype(jnp.bfloat16), "row", pairs), *marks) for part in sums]
            sums = [
                part.astype(jnp.float32) + other.astype(jnp.float32) for part, other in zip(sums, others)
            ]
        return sums

    helds = []
    for g in range(GROUPS):
        rows = slice(g * height, (g + 1) * height)
        own = jnp.stack([tokens[rows], cotangent[rows]])
        if g > 0:
            own = later(own, *ahead)
        for bit in outer:
            own = jnp.concatenate([own, swap(own, bit)], axis=1)
        if g > 0:
            own = later(own, *helds[-1])
        held, ahead = [], []
        for part, (start, stop) in enumerate(bounds):
            low = own[:, :, start:stop]
            rest = orders[part][len(outer) :]
            for bit in rest[:-1]:
                low = jnp.concatenate([low, swap(low, bit)], axis=1)
                if bit == rest[0]:
                    ahead.append(low)
            held.append(low)
        helds.append(held)
    for g, held in enumerate(helds):
        marks = helds[g + 1] if g + 1 < GROUPS else []
        helds[g] = [(low, swap(later(low, *marks), order[-1])) for low, order in zip(held, orders)]

    def stage(held, at, mark, marked):
        summed = []
        for part, (low, high) in enumerate(held):
            other = swap(high, orders[part][-1 - at])
            summed.append(add(low, other if mark is None or part >= marked else later(other, mark)))
        return summed

    def finish(summed, mark):
        total = jnp.concatenate(summed, axis=1)
        for bit in reversed(outer):
            low, high = halves(total)
            other = swap(high, bit)
            total = add(low, other if mark is None else later(other, mark))
        return total

    stages = len(orders[0]) - len(outer)
    last = GROUPS - 1
    fulls, actives, dhids, totals = [], [], [], []
    for g in range(GROUPS):
        after = [low for low, high in helds[g + 1]] if g + 1 < GROUPS else []
        after = after + ([half for pair in totals[-1] for half in pair] if g > 0 else [])
        full, *sums = forward(
            helds[g], orders, height, up_weight, down_weight, up_pattern, down_pattern, after
        )
        marks = [high for low, high in helds[g + 1][:2]] if g + 1 < GROUPS else []
        active, dhid = activate(*beside(sums, marks))
        fulls.append(full)
        actives.append(active)
        dhids.append(dhid)
        early, after = totals, []
        if g == last:
            for at, mark in zip(range(stages - 1), (sums[1], dhid)):
                early = [stage(held, at, mark, len(orders)) for held in early]
                after = [total for summed in early for total in summed]
                early = [[halves(total) for total in summed] for summed in early]
        totals.append(
            backward(dhid, up_weight, up_pattern, orders, height, bounds, after)
        )

    grads = [
        grad(fulls, dhids, up_pattern, block, (8, 12), 0, None, 2, False),
        grad(actives, fulls, down_pattern, block, (12, 8), None, 1, 2, True),
    ]
    work = [(which, call) for pair in zip(*grads) for which, call in enumerate(pair)]
    outs = [None, None]

    def advance(count, after):
        for which, call in work[:count]:
            outs[which] = call(outs[which], after)
        del work[:count]

    held = totals[last]
    advance(1, [half for pair in held for half in pair])
    late = [stage(pairs, stages - 1, outs[0], len(orders)) for pairs in early]
    advance(1, [total for summed in late for total in summed])
    shares = [finish(summed, outs[1]) for summed in late]
    for at in range(stages):
        summed = stage(held, at, outs[1 - at] if at < 2 else None, 2)
        if at == 0:
            advance(1, summed)
        if at < stages - 1:
            summed = lax.optimization_barrier(summed)
        held = [halves(total) for total in summed]
    advance(len(work), summed)
    shares.append(finish(summed, None))
    input_grad = jnp.concatenate(shares, axis=0)
    return (input_grad, outs[0], outs[1])


def solution(mesh):
    return jax.shard_map(
        functools.partial(on_device, dict(mesh.shape)),
        mesh=mesh,
        in_specs=(
            P("col", "row"),
            P("row", "col"),
            P("col", "row"),
            P("col", "row"),
            P("row", "col"),
            P("col", "row"),
        ),
        out_specs=(P("col", "row"), P("row", "col"), P("col", "row")),
        check_vma=False,
    )
```

```python
import functools

import jax
import jax.numpy as jnp
from jax import lax
from jax.experimental import pallas as pl
from jax.experimental.pallas import tpu as pltpu
from jax.sharding import PartitionSpec as P

half_root = 0.7071067811865476
inv_root_tau = 0.3989422804014327
GROUPS = 2
SPLIT = (18, 18)
OUT_OF = 48


def activate(pre, dact):
    cdf = 0.5 * (1.0 + jax.scipy.special.erf(pre * half_root))
    dens = jnp.exp(-0.5 * pre * pre) * inv_root_tau
    active = (pre * cdf).astype(jnp.bfloat16)
    dhid = (dact * (cdf + pre * dens)).astype(jnp.bfloat16)
    return (active, dhid)


def divisor(count, most):
    return max(k for k in range(1, most + 1) if count % k == 0)


def kept(flag, block):
    return jnp.where(flag != 0, block, jnp.zeros_like(block))


def runs(order, height, half):
    found = []
    for m in range(1 << len(order)):
        common = sum(((m >> k) & 1) << bit for k, bit in enumerate(order)) * height
        side, row = divmod(m * height, half)
        last = found[-1] if found else None
        if last and last[0] == side and last[2] + last[3] == common:
            last[3] += height
        else:
            found.append([side, row, common, height])
    return found


def forward_kernel(moves, block, up_on, down_on, *refs):
    arrays = 1 + max(move[0] for move in moves)
    held = refs[:arrays]
    up_hbm, down_hbm = refs[arrays : arrays + 2]
    full_hbm, *sum_hbm = refs[-11:-8]
    full, sums, up_buf, down_buf = refs[-8:-4]
    in_sems, out_sems, weight_sems, full_sem = refs[-4:]
    rows, width = full.shape[1:]
    columns, down = sums.shape[2] // block, width // block
    slots, each = up_buf.shape[0], up_buf.shape[2] // block
    turns = columns // each

    def here(turn):
        return pl.ds(pl.multiple_of(turn * each * block, each * block), each * block)

    def fetch(turn):
        slot = lax.rem(turn, slots)
        return (
            pltpu.make_async_copy(up_hbm.at[:, here(turn)], up_buf.at[slot], weight_sems.at[0, slot]),
            pltpu.make_async_copy(down_hbm.at[here(turn), :], down_buf.at[slot], weight_sems.at[1, slot]),
        )

    copies = [
        pltpu.make_async_copy(
            held[array].at[:, pl.ds(source, tall), :],
            full.at[:, pl.ds(target, tall), pl.ds(lane, breadth)],
            in_sems.at[at],
        )
        for at, (array, source, target, tall, lane, breadth) in enumerate(moves)
    ]
    for copy in copies:
        copy.start()
    for turn in range(min(slots, turns)):
        for copy in fetch(turn):
            copy.start()
    for copy in copies:
        copy.wait()
    whole = pltpu.make_async_copy(full, full_hbm, full_sem)
    whole.start()

    def leave(turn):
        return [
            pltpu.make_async_copy(
                sums.at[w, :, here(turn)], sum_hbm[w].at[:, here(turn)], out_sems.at[w, turn]
            )
            for w in range(2)
        ]

    def step(turn, carry):
        lanes = here(turn)
        slot = lax.rem(turn, slots)
        for copy in fetch(turn):
            copy.wait()
        right = jnp.concatenate(
            [
                jnp.concatenate(
                    [
                        kept(
                            up_on[i, turn * each + c],
                            up_buf[slot, i * block : (i + 1) * block, c * block : (c + 1) * block],
                        )
                        for c in range(each)
                    ],
                    1,
                )
                for i in range(down)
            ],
            0,
        )
        pre = jnp.dot(full[0], right, preferred_element_type=jnp.float32)
        sums[0, :, lanes] = pre.astype(jnp.bfloat16)
        right = jnp.concatenate(
            [
                jnp.concatenate(
                    [
                        kept(
                            down_on[turn * each + c, i],
                            down_buf[
                                slot, c * block : (c + 1) * block, i * block : (i + 1) * block
                            ],
                        )
                        for i in range(down)
                    ],
                    1,
                )
                for c in range(each)
            ],
            0,
        )
        dact = lax.dot_general(
            full[1], right, (((1,), (1,)), ((), ())), preferred_element_type=jnp.float32
        )
        sums[1, :, lanes] = dact.astype(jnp.bfloat16)

        @pl.when(turn + slots < turns)
        def _():
            for copy in fetch(turn + slots):
                copy.start()

        for copy in leave(turn):
            copy.start()
        return carry

    lax.fori_loop(0, turns, step, 0)
    for turn in range(turns):
        for copy in leave(turn):
            copy.wait()
    whole.wait()


def forward(held, orders, height, up_weight, down_weight, up_on, down_on, after):
    width, hidden = up_weight.shape
    block = width // up_on.shape[0]
    rows = 2 * held[0][0].shape[1]
    moves, arrays, lane = [], [], 0
    for (low, high), order in zip(held, orders):
        for side, source, target, tall in runs(order, height, rows // 2):
            moves.append((len(arrays) + side, source, target, tall, lane, low.shape[2]))
        arrays += [low, high]
        lane += low.shape[2]
    any_space = pl.BlockSpec(memory_space=pl.ANY)
    smem = pl.BlockSpec(memory_space=pltpu.SMEM)
    each = divisor(hidden // block, 2)
    slots = 3
    shapes = [
        ((2, rows, width), jnp.bfloat16),
        ((2, rows, hidden), jnp.bfloat16),
    ]
    return pl.pallas_call(
        functools.partial(forward_kernel, moves, block),
        in_specs=[smem] * 2 + [any_space] * (len(arrays) + 2 + len(after)),
        out_specs=[any_space] * 3,
        scratch_shapes=[pltpu.VMEM(*shape) for shape in shapes]
        + [
            pltpu.VMEM((slots, width, each * block), jnp.bfloat16),
            pltpu.VMEM((slots, each * block, width), jnp.bfloat16),
            pltpu.SemaphoreType.DMA((len(moves),)),
            pltpu.SemaphoreType.DMA((2, hidden // block // each)),
            pltpu.SemaphoreType.DMA((2, slots)),
            pltpu.SemaphoreType.DMA,
        ],
        out_shape=[jax.ShapeDtypeStruct(*shape) for shape in shapes[:1]]
        + [jax.ShapeDtypeStruct((rows, hidden), jnp.bfloat16)] * 2,
        compiler_params=pltpu.CompilerParams(vmem_limit_bytes=48 * 1024 * 1024),
        cost_estimate=pl.CostEstimate(
            flops=rows * width, bytes_accessed=rows * width, transcendentals=0
        ),
        name="forward",
    )(up_on, down_on, *arrays, up_weight, down_weight, *after)


def backward_kernel(parts, block, up_on, dhid_ref, up_hbm, *refs):
    outs, (buf, sems) = refs[-2 - 2 * len(parts) : -2], refs[-2:]
    across = up_hbm.shape[1] // block
    tiles, at = [], 0
    for part, (moves, count) in enumerate(parts):
        each = divisor(count, 6)
        tiles += [(part, moves, at + r, r, each) for r in range(0, count, each)]
        at += count
    copies = []
    for k, (part, moves, row, lane, each) in enumerate(tiles):
        rows = pl.ds(row * block, each * block)
        copies.append(pltpu.make_async_copy(up_hbm.at[rows, :], buf.at[rows, :], sems.at[k]))
    for copy in copies:
        copy.start()
    for copy, (part, moves, row, lane, each) in zip(copies, tiles):
        copy.wait()
        right = jnp.concatenate(
            [
                jnp.concatenate(
                    [
                        kept(
                            up_on[row + r, c],
                            buf[(row + r) * block : (row + r + 1) * block, c * block : (c + 1) * block],
                        )
                        for c in range(across)
                    ],
                    1,
                )
                for r in range(each)
            ],
            0,
        )
        acc = lax.dot_general(
            dhid_ref[...], right, (((1,), (1,)), ((), ())), preferred_element_type=jnp.float32
        ).astype(jnp.bfloat16)
        for side, target, source, tall in moves:
            outs[2 * part + side][
                target : target + tall, lane * block : (lane + each) * block
            ] = acc[source : source + tall]


def backward(dhid, up_weight, up_on, orders, height, bounds, after):
    width, hidden = up_weight.shape
    block = width // up_on.shape[0]
    rows = dhid.shape[0]
    parts = [
        (runs(order, height, rows // 2), (stop - start) // block)
        for order, (start, stop) in zip(orders, bounds)
    ]
    tiles = sum(count // divisor(count, 6) for moves, count in parts)
    vmem = pl.BlockSpec(memory_space=pltpu.VMEM)
    smem = pl.BlockSpec(memory_space=pltpu.SMEM)
    any_space = pl.BlockSpec(memory_space=pl.ANY)
    outs = pl.pallas_call(
        functools.partial(backward_kernel, parts, block),
        in_specs=[smem, vmem] + [any_space] * (1 + len(after)),
        out_specs=[vmem] * (2 * len(parts)),
        scratch_shapes=[pltpu.VMEM((width, hidden), jnp.bfloat16), pltpu.SemaphoreType.DMA((tiles,))],
        out_shape=[
            jax.ShapeDtypeStruct((rows // 2, count * block), jnp.bfloat16)
            for moves, count in parts
            for side in range(2)
        ],
        compiler_params=pltpu.CompilerParams(vmem_limit_bytes=48 * 1024 * 1024),
        cost_estimate=pl.CostEstimate(
            flops=rows * width, bytes_accessed=rows * width, transcendentals=0
        ),
        name="backward",
    )(up_on, dhid, up_weight, *after)
    return [(outs[2 * part], outs[2 * part + 1]) for part in range(len(parts))]


def grad_kernel(block, factor, first, groups, pattern, *refs):
    lefts, rights, out_ref = refs[:groups], refs[groups : 2 * groups], refs[-1]
    down, across = out_ref.shape[0] // block, out_ref.shape[1] // block
    row = first[0] + pl.program_id(0) * down
    column = first[1] + pl.program_id(1) * across
    chunk = 2 if across % 2 == 0 else 1
    left = jnp.concatenate([ref[...] for ref in lefts], axis=0)
    for c in range(0, across, chunk):
        lanes = slice(c * block, (c + chunk) * block)
        acc = lax.dot_general(
            left,
            jnp.concatenate([ref[:, lanes] for ref in rights], axis=0),
            (((0,), (0,)), ((), ())),
            preferred_element_type=jnp.float32,
        )
        for r in range(down):
            for q in range(chunk):
                scale = jnp.where(pattern[row + r, column + c + q] != 0, factor, 0.0)
                out_ref[r * block : (r + 1) * block, (c + q) * block : (c + q + 1) * block] = (
                    acc[r * block : (r + 1) * block, q * block : (q + 1) * block] * scale
                ).astype(jnp.bfloat16)


def grad(lefts, rights, pattern, block, most, left_which, right_which, shares, by_column):
    groups = len(lefts)
    tall, broad = lefts[0].shape[-1], rights[0].shape[-1]
    tile = (
        divisor(tall // block // (1 if by_column else shares), most[0]) * block,
        divisor(broad // block // (shares if by_column else 1), most[1]) * block,
    )
    rows = lefts[0].shape[-2]
    tokens = groups * rows
    factor = float(1.0 / tokens**0.5)
    steps = [tall // tile[0], broad // tile[1]]
    steps[int(by_column)] //= shares

    def spec(which, breadth, index):
        if which is None:
            return pl.BlockSpec((rows, breadth), lambda i, c, *_: (0, index(i, c)))
        return pl.BlockSpec((None, rows, breadth), lambda i, c, *_: (which, 0, index(i, c)))

    def make(share):
        off = (0, share * steps[1]) if by_column else (share * steps[0], 0)

        def call(out, after):
            in_specs = [spec(left_which, tile[0], lambda i, c: off[0] + i)] * groups
            in_specs += [spec(right_which, tile[1], lambda i, c: off[1] + c)] * groups
            args = [*lefts, *rights, *after]
            in_specs += [pl.BlockSpec(memory_space=pl.ANY)] * len(after)
            aliases = {}
            if out is not None:
                in_specs.append(pl.BlockSpec(memory_space=pl.ANY))
                args.append(out)
                aliases = {len(args): 0}
            return pl.pallas_call(
                functools.partial(
                    grad_kernel,
                    block,
                    factor,
                    (off[0] * tile[0] // block, off[1] * tile[1] // block),
                    groups,
                ),
                grid_spec=pltpu.PrefetchScalarGridSpec(
                    num_scalar_prefetch=1,
                    grid=tuple(steps),
                    in_specs=in_specs,
                    out_specs=pl.BlockSpec(tile, lambda i, c, *_: (off[0] + i, off[1] + c)),
                ),
                out_shape=jax.ShapeDtypeStruct((tall, broad), jnp.bfloat16),
                input_output_aliases=aliases,
                compiler_params=pltpu.CompilerParams(vmem_limit_bytes=32 * 1024 * 1024),
                cost_estimate=pl.CostEstimate(
                    flops=tall * broad // shares,
                    bytes_accessed=tokens * broad // shares,
                    transcendentals=0,
                ),
                name="grad",
            )(pattern, *args)

        return call

    return [make(share) for share in range(shares)]


def add(left, right):
    return (left.astype(jnp.float32) + right.astype(jnp.float32)).astype(jnp.bfloat16)


def halves(value):
    half = value.shape[0] // 2
    return (value[:half], value[half:])


def on_device(sizes, tokens, up_weight, down_weight, cotangent, up_pattern, down_pattern):
    n, across = sizes["col"], sizes["row"]
    bits = n.bit_length() - 1
    far = list(range(bits - 1, 1, -1))
    outer, near = far[:-1], far[-1:]
    orders = [[*outer, 1, *near, 0], [*outer, *near, 0, 1], [*outer, 0, 1, *near]]
    width, hidden = up_weight.shape
    down = up_pattern.shape[0]
    block = width // down
    height = tokens.shape[0] // GROUPS
    bounds = [0, SPLIT[0] * down // OUT_OF, sum(SPLIT) * down // OUT_OF, down]
    bounds = [(at * block, to * block) for at, to in zip(bounds, bounds[1:])]

    def swap(value, bit):
        return lax.ppermute(value, "col", [(i, i ^ (1 << bit)) for i in range(n)])

    def later(value, *marks):
        return lax.optimization_barrier((value, *marks))[0]

    def beside(sums, marks):
        for bit in range(across.bit_length() - 1):
            pairs = [(i, i ^ (1 << bit)) for i in range(across)]
            others = [later(lax.ppermute(part.astype(jnp.bfloat16), "row", pairs), *marks) for part in sums]
            sums = [
                part.astype(jnp.float32) + other.astype(jnp.float32) for part, other in zip(sums, others)
            ]
        return sums

    helds = []
    for g in range(GROUPS):
        rows = slice(g * height, (g + 1) * height)
        own = jnp.stack([tokens[rows], cotangent[rows]])
        if g > 0:
            own = later(own, *ahead)
        for bit in outer:
            own = jnp.concatenate([own, swap(own, bit)], axis=1)
        if g > 0:
            own = later(own, *helds[-1])
        held, ahead = [], []
        for part, (start, stop) in enumerate(bounds):
            low = own[:, :, start:stop]
            rest = orders[part][len(outer) :]
            for bit in rest[:-1]:
                low = jnp.concatenate([low, swap(low, bit)], axis=1)
                if bit == rest[0]:
                    ahead.append(low)
            held.append(low)
        helds.append(held)
    for g, held in enumerate(helds):
        marks = helds[g + 1] if g + 1 < GROUPS else []
        helds[g] = [(low, swap(later(low, *marks), order[-1])) for low, order in zip(held, orders)]

    def stage(held, at, mark, marked):
        summed = []
        for part, (low, high) in enumerate(held):
            other = swap(high, orders[part][-1 - at])
            summed.append(add(low, other if mark is None or part >= marked else later(other, mark)))
        return summed

    def finish(summed, mark):
        total = jnp.concatenate(summed, axis=1)
        for bit in reversed(outer):
            low, high = halves(total)
            other = swap(high, bit)
            total = add(low, other if mark is None else later(other, mark))
        return total

    stages = len(orders[0]) - len(outer)
    last = GROUPS - 1
    fulls, actives, dhids, totals = [], [], [], []
    for g in range(GROUPS):
        after = [low for low, high in helds[g + 1]] if g + 1 < GROUPS else []
        after = after + ([half for pair in totals[-1] for half in pair] if g > 0 else [])
        full, *sums = forward(
            helds[g], orders, height, up_weight, down_weight, up_pattern, down_pattern, after
        )
        marks = [high for low, high in helds[g + 1][:2]] if g + 1 < GROUPS else []
        active, dhid = activate(*beside(sums, marks))
        fulls.append(full)
        actives.append(active)
        dhids.append(dhid)
        early, after = totals, []
        if g == last:
            for at, mark in zip(range(stages - 1), (sums[1], dhid)):
                early = [stage(held, at, mark, len(orders)) for held in early]
                after = [total for summed in early for total in summed]
                early = [[halves(total) for total in summed] for summed in early]
        totals.append(
            backward(dhid, up_weight, up_pattern, orders, height, bounds, after)
        )

    grads = [
        grad(fulls, dhids, up_pattern, block, (8, 12), 0, None, 2, False),
        grad(actives, fulls, down_pattern, block, (12, 8), None, 1, 2, True),
    ]
    work = [(which, call) for pair in zip(*grads) for which, call in enumerate(pair)]
    outs = [None, None]

    def advance(count, after):
        for which, call in work[:count]:
            outs[which] = call(outs[which], after)
        del work[:count]

    held = totals[last]
    advance(2, [half for pair in held for half in pair])
    late = [stage(pairs, stages - 1, outs[1], len(orders)) for pairs in early]
    for at in range(stages):
        summed = stage(held, at, outs[1 - at] if at < 2 else None, 2)
        if at == 0:
            advance(1, summed)
            shares = [finish(done, outs[0]) for done in late]
        if at < stages - 1:
            summed = lax.optimization_barrier(summed)
        held = [halves(total) for total in summed]
    advance(len(work), summed)
    shares.append(finish(summed, None))
    input_grad = jnp.concatenate(shares, axis=0)
    return (input_grad, outs[0], outs[1])


def solution(mesh):
    return jax.shard_map(
        functools.partial(on_device, dict(mesh.shape)),
        mesh=mesh,
        in_specs=(
            P("col", "row"),
            P("row", "col"),
            P("col", "row"),
            P("col", "row"),
            P("row", "col"),
            P("col", "row"),
        ),
        out_specs=(P("col", "row"), P("row", "col"), P("col", "row")),
        check_vma=False,
    )
```

```python
import functools

import jax
import jax.numpy as jnp
from jax import lax
from jax.experimental import pallas as pl
from jax.experimental.pallas import tpu as pltpu
from jax.sharding import PartitionSpec as P

half_root = 0.7071067811865476
inv_root_tau = 0.3989422804014327
GROUPS = 2
SPLIT = (18, 20)
OUT_OF = 48


def activate(pre, dact):
    cdf = 0.5 * (1.0 + jax.scipy.special.erf(pre * half_root))
    dens = jnp.exp(-0.5 * pre * pre) * inv_root_tau
    active = (pre * cdf).astype(jnp.bfloat16)
    dhid = (dact * (cdf + pre * dens)).astype(jnp.bfloat16)
    return (active, dhid)


def divisor(count, most):
    return max(k for k in range(1, most + 1) if count % k == 0)


def kept(flag, block):
    return jnp.where(flag != 0, block, jnp.zeros_like(block))


def runs(order, height, half):
    found = []
    for m in range(1 << len(order)):
        common = sum(((m >> k) & 1) << bit for k, bit in enumerate(order)) * height
        side, row = divmod(m * height, half)
        last = found[-1] if found else None
        if last and last[0] == side and last[2] + last[3] == common:
            last[3] += height
        else:
            found.append([side, row, common, height])
    return found


def forward_kernel(moves, block, up_on, down_on, *refs):
    arrays = 1 + max(move[0] for move in moves)
    held = refs[:arrays]
    up_hbm, down_hbm = refs[arrays : arrays + 2]
    full_hbm, *sum_hbm = refs[-11:-8]
    full, sums, up_buf, down_buf = refs[-8:-4]
    in_sems, out_sems, weight_sems, full_sem = refs[-4:]
    rows, width = full.shape[1:]
    columns, down = sums.shape[2] // block, width // block
    slots, each = up_buf.shape[0], up_buf.shape[2] // block
    turns = columns // each

    def here(turn):
        return pl.ds(pl.multiple_of(turn * each * block, each * block), each * block)

    def fetch(turn):
        slot = lax.rem(turn, slots)
        return (
            pltpu.make_async_copy(up_hbm.at[:, here(turn)], up_buf.at[slot], weight_sems.at[0, slot]),
            pltpu.make_async_copy(down_hbm.at[here(turn), :], down_buf.at[slot], weight_sems.at[1, slot]),
        )

    copies = [
        pltpu.make_async_copy(
            held[array].at[:, pl.ds(source, tall), :],
            full.at[:, pl.ds(target, tall), pl.ds(lane, breadth)],
            in_sems.at[at],
        )
        for at, (array, source, target, tall, lane, breadth) in enumerate(moves)
    ]
    for copy in copies:
        copy.start()
    for turn in range(min(slots, turns)):
        for copy in fetch(turn):
            copy.start()
    for copy in copies:
        copy.wait()
    whole = pltpu.make_async_copy(full, full_hbm, full_sem)
    whole.start()

    def leave(turn):
        return [
            pltpu.make_async_copy(
                sums.at[w, :, here(turn)], sum_hbm[w].at[:, here(turn)], out_sems.at[w, turn]
            )
            for w in range(2)
        ]

    def step(turn, carry):
        lanes = here(turn)
        slot = lax.rem(turn, slots)
        for copy in fetch(turn):
            copy.wait()
        right = jnp.concatenate(
            [
                jnp.concatenate(
                    [
                        kept(
                            up_on[i, turn * each + c],
                            up_buf[slot, i * block : (i + 1) * block, c * block : (c + 1) * block],
                        )
                        for c in range(each)
                    ],
                    1,
                )
                for i in range(down)
            ],
            0,
        )
        pre = jnp.dot(full[0], right, preferred_element_type=jnp.float32)
        sums[0, :, lanes] = pre.astype(jnp.bfloat16)
        right = jnp.concatenate(
            [
                jnp.concatenate(
                    [
                        kept(
                            down_on[turn * each + c, i],
                            down_buf[
                                slot, c * block : (c + 1) * block, i * block : (i + 1) * block
                            ],
                        )
                        for i in range(down)
                    ],
                    1,
                )
                for c in range(each)
            ],
            0,
        )
        dact = lax.dot_general(
            full[1], right, (((1,), (1,)), ((), ())), preferred_element_type=jnp.float32
        )
        sums[1, :, lanes] = dact.astype(jnp.bfloat16)

        @pl.when(turn + slots < turns)
        def _():
            for copy in fetch(turn + slots):
                copy.start()

        for copy in leave(turn):
            copy.start()
        return carry

    lax.fori_loop(0, turns, step, 0)
    for turn in range(turns):
        for copy in leave(turn):
            copy.wait()
    whole.wait()


def forward(held, orders, height, up_weight, down_weight, up_on, down_on, after):
    width, hidden = up_weight.shape
    block = width // up_on.shape[0]
    rows = 2 * held[0][0].shape[1]
    moves, arrays, lane = [], [], 0
    for (low, high), order in zip(held, orders):
        for side, source, target, tall in runs(order, height, rows // 2):
            moves.append((len(arrays) + side, source, target, tall, lane, low.shape[2]))
        arrays += [low, high]
        lane += low.shape[2]
    any_space = pl.BlockSpec(memory_space=pl.ANY)
    smem = pl.BlockSpec(memory_space=pltpu.SMEM)
    each = divisor(hidden // block, 2)
    slots = 3
    shapes = [
        ((2, rows, width), jnp.bfloat16),
        ((2, rows, hidden), jnp.bfloat16),
    ]
    return pl.pallas_call(
        functools.partial(forward_kernel, moves, block),
        in_specs=[smem] * 2 + [any_space] * (len(arrays) + 2 + len(after)),
        out_specs=[any_space] * 3,
        scratch_shapes=[pltpu.VMEM(*shape) for shape in shapes]
        + [
            pltpu.VMEM((slots, width, each * block), jnp.bfloat16),
            pltpu.VMEM((slots, each * block, width), jnp.bfloat16),
            pltpu.SemaphoreType.DMA((len(moves),)),
            pltpu.SemaphoreType.DMA((2, hidden // block // each)),
            pltpu.SemaphoreType.DMA((2, slots)),
            pltpu.SemaphoreType.DMA,
        ],
        out_shape=[jax.ShapeDtypeStruct(*shape) for shape in shapes[:1]]
        + [jax.ShapeDtypeStruct((rows, hidden), jnp.bfloat16)] * 2,
        compiler_params=pltpu.CompilerParams(vmem_limit_bytes=48 * 1024 * 1024),
        cost_estimate=pl.CostEstimate(
            flops=rows * width, bytes_accessed=rows * width, transcendentals=0
        ),
        name="forward",
    )(up_on, down_on, *arrays, up_weight, down_weight, *after)


def backward_kernel(parts, block, up_on, dhid_ref, up_hbm, *refs):
    outs, (buf, sems) = refs[-2 - 2 * len(parts) : -2], refs[-2:]
    across = up_hbm.shape[1] // block
    tiles, at = [], 0
    for part, (moves, count) in enumerate(parts):
        each = divisor(count, 6)
        tiles += [(part, moves, at + r, r, each) for r in range(0, count, each)]
        at += count
    copies = []
    for k, (part, moves, row, lane, each) in enumerate(tiles):
        rows = pl.ds(row * block, each * block)
        copies.append(pltpu.make_async_copy(up_hbm.at[rows, :], buf.at[rows, :], sems.at[k]))
    for copy in copies:
        copy.start()
    for copy, (part, moves, row, lane, each) in zip(copies, tiles):
        copy.wait()
        right = jnp.concatenate(
            [
                jnp.concatenate(
                    [
                        kept(
                            up_on[row + r, c],
                            buf[(row + r) * block : (row + r + 1) * block, c * block : (c + 1) * block],
                        )
                        for c in range(across)
                    ],
                    1,
                )
                for r in range(each)
            ],
            0,
        )
        acc = lax.dot_general(
            dhid_ref[...], right, (((1,), (1,)), ((), ())), preferred_element_type=jnp.float32
        ).astype(jnp.bfloat16)
        for side, target, source, tall in moves:
            outs[2 * part + side][
                target : target + tall, lane * block : (lane + each) * block
            ] = acc[source : source + tall]


def backward(dhid, up_weight, up_on, orders, height, bounds, after):
    width, hidden = up_weight.shape
    block = width // up_on.shape[0]
    rows = dhid.shape[0]
    parts = [
        (runs(order, height, rows // 2), (stop - start) // block)
        for order, (start, stop) in zip(orders, bounds)
    ]
    tiles = sum(count // divisor(count, 6) for moves, count in parts)
    vmem = pl.BlockSpec(memory_space=pltpu.VMEM)
    smem = pl.BlockSpec(memory_space=pltpu.SMEM)
    any_space = pl.BlockSpec(memory_space=pl.ANY)
    outs = pl.pallas_call(
        functools.partial(backward_kernel, parts, block),
        in_specs=[smem, vmem] + [any_space] * (1 + len(after)),
        out_specs=[vmem] * (2 * len(parts)),
        scratch_shapes=[pltpu.VMEM((width, hidden), jnp.bfloat16), pltpu.SemaphoreType.DMA((tiles,))],
        out_shape=[
            jax.ShapeDtypeStruct((rows // 2, count * block), jnp.bfloat16)
            for moves, count in parts
            for side in range(2)
        ],
        compiler_params=pltpu.CompilerParams(vmem_limit_bytes=48 * 1024 * 1024),
        cost_estimate=pl.CostEstimate(
            flops=rows * width, bytes_accessed=rows * width, transcendentals=0
        ),
        name="backward",
    )(up_on, dhid, up_weight, *after)
    return [(outs[2 * part], outs[2 * part + 1]) for part in range(len(parts))]


def grad_kernel(block, factor, first, groups, pattern, *refs):
    lefts, rights, out_ref = refs[:groups], refs[groups : 2 * groups], refs[-1]
    down, across = out_ref.shape[0] // block, out_ref.shape[1] // block
    row = first[0] + pl.program_id(0) * down
    column = first[1] + pl.program_id(1) * across
    chunk = 2 if across % 2 == 0 else 1
    left = jnp.concatenate([ref[...] for ref in lefts], axis=0)
    for c in range(0, across, chunk):
        lanes = slice(c * block, (c + chunk) * block)
        acc = lax.dot_general(
            left,
            jnp.concatenate([ref[:, lanes] for ref in rights], axis=0),
            (((0,), (0,)), ((), ())),
            preferred_element_type=jnp.float32,
        )
        for r in range(down):
            for q in range(chunk):
                scale = jnp.where(pattern[row + r, column + c + q] != 0, factor, 0.0)
                out_ref[r * block : (r + 1) * block, (c + q) * block : (c + q + 1) * block] = (
                    acc[r * block : (r + 1) * block, q * block : (q + 1) * block] * scale
                ).astype(jnp.bfloat16)


def grad(lefts, rights, pattern, block, most, left_which, right_which, shares, by_column):
    groups = len(lefts)
    tall, broad = lefts[0].shape[-1], rights[0].shape[-1]
    tile = (
        divisor(tall // block // (1 if by_column else shares), most[0]) * block,
        divisor(broad // block // (shares if by_column else 1), most[1]) * block,
    )
    rows = lefts[0].shape[-2]
    tokens = groups * rows
    factor = float(1.0 / tokens**0.5)
    steps = [tall // tile[0], broad // tile[1]]
    steps[int(by_column)] //= shares

    def spec(which, breadth, index):
        if which is None:
            return pl.BlockSpec((rows, breadth), lambda i, c, *_: (0, index(i, c)))
        return pl.BlockSpec((None, rows, breadth), lambda i, c, *_: (which, 0, index(i, c)))

    def make(share):
        off = (0, share * steps[1]) if by_column else (share * steps[0], 0)

        def call(out, after):
            in_specs = [spec(left_which, tile[0], lambda i, c: off[0] + i)] * groups
            in_specs += [spec(right_which, tile[1], lambda i, c: off[1] + c)] * groups
            args = [*lefts, *rights, *after]
            in_specs += [pl.BlockSpec(memory_space=pl.ANY)] * len(after)
            aliases = {}
            if out is not None:
                in_specs.append(pl.BlockSpec(memory_space=pl.ANY))
                args.append(out)
                aliases = {len(args): 0}
            return pl.pallas_call(
                functools.partial(
                    grad_kernel,
                    block,
                    factor,
                    (off[0] * tile[0] // block, off[1] * tile[1] // block),
                    groups,
                ),
                grid_spec=pltpu.PrefetchScalarGridSpec(
                    num_scalar_prefetch=1,
                    grid=tuple(steps),
                    in_specs=in_specs,
                    out_specs=pl.BlockSpec(tile, lambda i, c, *_: (off[0] + i, off[1] + c)),
                ),
                out_shape=jax.ShapeDtypeStruct((tall, broad), jnp.bfloat16),
                input_output_aliases=aliases,
                compiler_params=pltpu.CompilerParams(vmem_limit_bytes=32 * 1024 * 1024),
                cost_estimate=pl.CostEstimate(
                    flops=tall * broad // shares,
                    bytes_accessed=tokens * broad // shares,
                    transcendentals=0,
                ),
                name="grad",
            )(pattern, *args)

        return call

    return [make(share) for share in range(shares)]


def add(left, right):
    return (left.astype(jnp.float32) + right.astype(jnp.float32)).astype(jnp.bfloat16)


def halves(value):
    half = value.shape[0] // 2
    return (value[:half], value[half:])


def on_device(sizes, tokens, up_weight, down_weight, cotangent, up_pattern, down_pattern):
    n, across = sizes["col"], sizes["row"]
    bits = n.bit_length() - 1
    far = list(range(bits - 1, 1, -1))
    outer, near = far[:-1], far[-1:]
    orders = [[*outer, 1, *near, 0], [*outer, *near, 0, 1], [*outer, 0, 1, *near]]
    width, hidden = up_weight.shape
    down = up_pattern.shape[0]
    block = width // down
    height = tokens.shape[0] // GROUPS
    bounds = [0, SPLIT[0] * down // OUT_OF, sum(SPLIT) * down // OUT_OF, down]
    bounds = [(at * block, to * block) for at, to in zip(bounds, bounds[1:])]

    def swap(value, bit):
        return lax.ppermute(value, "col", [(i, i ^ (1 << bit)) for i in range(n)])

    def later(value, *marks):
        return lax.optimization_barrier((value, *marks))[0]

    def beside(sums, marks):
        for bit in range(across.bit_length() - 1):
            pairs = [(i, i ^ (1 << bit)) for i in range(across)]
            others = [later(lax.ppermute(part.astype(jnp.bfloat16), "row", pairs), *marks) for part in sums]
            sums = [
                part.astype(jnp.float32) + other.astype(jnp.float32) for part, other in zip(sums, others)
            ]
        return sums

    helds = []
    for g in range(GROUPS):
        rows = slice(g * height, (g + 1) * height)
        own = jnp.stack([tokens[rows], cotangent[rows]])
        if g > 0:
            own = later(own, *ahead)
        for bit in outer:
            own = jnp.concatenate([own, swap(own, bit)], axis=1)
        if g > 0:
            own = later(own, *helds[-1])
        held, ahead = [], []
        for part, (start, stop) in enumerate(bounds):
            low = own[:, :, start:stop]
            rest = orders[part][len(outer) :]
            for bit in rest[:-1]:
                low = jnp.concatenate([low, swap(low, bit)], axis=1)
                if bit == rest[0]:
                    ahead.append(low)
            held.append(low)
        helds.append(held)
    for g, held in enumerate(helds):
        marks = helds[g + 1] if g + 1 < GROUPS else []
        helds[g] = [(low, swap(later(low, *marks), order[-1])) for low, order in zip(held, orders)]

    def stage(held, at, mark, marked):
        summed = []
        for part, (low, high) in enumerate(held):
            other = swap(high, orders[part][-1 - at])
            summed.append(add(low, other if mark is None or part >= marked else later(other, mark)))
        return summed

    def finish(summed, mark):
        total = jnp.concatenate(summed, axis=1)
        for bit in reversed(outer):
            low, high = halves(total)
            other = swap(high, bit)
            total = add(low, other if mark is None else later(other, mark))
        return total

    stages = len(orders[0]) - len(outer)
    last = GROUPS - 1
    fulls, actives, dhids, totals = [], [], [], []
    for g in range(GROUPS):
        after = [low for low, high in helds[g + 1]] if g + 1 < GROUPS else []
        after = after + ([half for pair in totals[-1] for half in pair] if g > 0 else [])
        full, *sums = forward(
            helds[g], orders, height, up_weight, down_weight, up_pattern, down_pattern, after
        )
        marks = [high for low, high in helds[g + 1][:2]] if g + 1 < GROUPS else []
        active, dhid = activate(*beside(sums, marks))
        fulls.append(full)
        actives.append(active)
        dhids.append(dhid)
        early, after = totals, []
        if g == last:
            for at, mark in zip(range(stages - 1), (sums[1], dhid)):
                early = [stage(held, at, mark, len(orders)) for held in early]
                after = [total for summed in early for total in summed]
                early = [[halves(total) for total in summed] for summed in early]
        totals.append(
            backward(dhid, up_weight, up_pattern, orders, height, bounds, after)
        )

    grads = [
        grad(fulls, dhids, up_pattern, block, (8, 12), 0, None, 2, False),
        grad(actives, fulls, down_pattern, block, (12, 8), None, 1, 2, True),
    ]
    work = [(which, call) for pair in zip(*grads) for which, call in enumerate(pair)]
    outs = [None, None]

    def advance(count, after):
        for which, call in work[:count]:
            outs[which] = call(outs[which], after)
        del work[:count]

    held = totals[last]
    advance(2, [half for pair in held for half in pair])
    late = [stage(pairs, stages - 1, outs[1], len(orders)) for pairs in early]
    for at in range(stages):
        summed = stage(held, at, outs[1 - at] if at < 2 else None, 2)
        if at == 0:
            advance(1, summed)
            shares = [finish(done, outs[0]) for done in late]
        if at < stages - 1:
            summed = lax.optimization_barrier(summed)
        held = [halves(total) for total in summed]
    advance(len(work), summed)
    shares.append(finish(summed, None))
    input_grad = jnp.concatenate(shares, axis=0)
    return (input_grad, outs[0], outs[1])


def solution(mesh):
    return jax.shard_map(
        functools.partial(on_device, dict(mesh.shape)),
        mesh=mesh,
        in_specs=(
            P("col", "row"),
            P("row", "col"),
            P("col", "row"),
            P("col", "row"),
            P("row", "col"),
            P("col", "row"),
        ),
        out_specs=(P("col", "row"), P("row", "col"), P("col", "row")),
        check_vma=False,
    )
```

```python
import functools

import jax
import jax.numpy as jnp
from jax import lax
from jax.experimental import pallas as pl
from jax.experimental.pallas import tpu as pltpu
from jax.sharding import PartitionSpec as P

half_root = 0.7071067811865476
inv_root_tau = 0.3989422804014327
GROUPS = 2
SPLIT = (18, 20)
OUT_OF = 48


def activate(pre, dact):
    cdf = 0.5 * (1.0 + jax.scipy.special.erf(pre * half_root))
    dens = jnp.exp(-0.5 * pre * pre) * inv_root_tau
    active = (pre * cdf).astype(jnp.bfloat16)
    dhid = (dact * (cdf + pre * dens)).astype(jnp.bfloat16)
    return (active, dhid)


def divisor(count, most):
    return max(k for k in range(1, most + 1) if count % k == 0)


def kept(flag, block):
    return jnp.where(flag != 0, block, jnp.zeros_like(block))


def runs(order, height, half):
    found = []
    for m in range(1 << len(order)):
        common = sum(((m >> k) & 1) << bit for k, bit in enumerate(order)) * height
        side, row = divmod(m * height, half)
        last = found[-1] if found else None
        if last and last[0] == side and last[2] + last[3] == common:
            last[3] += height
        else:
            found.append([side, row, common, height])
    return found


def forward_kernel(moves, block, up_on, down_on, *refs):
    arrays = 1 + max(move[0] for move in moves)
    held = refs[:arrays]
    up_hbm, down_hbm = refs[arrays : arrays + 2]
    full_hbm, *sum_hbm = refs[-11:-8]
    full, sums, up_buf, down_buf = refs[-8:-4]
    in_sems, out_sems, weight_sems, full_sem = refs[-4:]
    rows, width = full.shape[1:]
    columns, down = sums.shape[2] // block, width // block
    slots, each = up_buf.shape[0], up_buf.shape[2] // block
    turns = columns // each

    def here(turn):
        return pl.ds(pl.multiple_of(turn * each * block, each * block), each * block)

    def fetch(turn):
        slot = lax.rem(turn, slots)
        return (
            pltpu.make_async_copy(up_hbm.at[:, here(turn)], up_buf.at[slot], weight_sems.at[0, slot]),
            pltpu.make_async_copy(down_hbm.at[here(turn), :], down_buf.at[slot], weight_sems.at[1, slot]),
        )

    copies = [
        pltpu.make_async_copy(
            held[array].at[:, pl.ds(source, tall), :],
            full.at[:, pl.ds(target, tall), pl.ds(lane, breadth)],
            in_sems.at[at],
        )
        for at, (array, source, target, tall, lane, breadth) in enumerate(moves)
    ]
    for copy in copies:
        copy.start()
    for turn in range(min(slots, turns)):
        for copy in fetch(turn):
            copy.start()
    for copy in copies:
        copy.wait()
    whole = pltpu.make_async_copy(full, full_hbm, full_sem)
    whole.start()

    def leave(turn):
        return [
            pltpu.make_async_copy(
                sums.at[w, :, here(turn)], sum_hbm[w].at[:, here(turn)], out_sems.at[w, turn]
            )
            for w in range(2)
        ]

    def step(turn, carry):
        lanes = here(turn)
        slot = lax.rem(turn, slots)
        for copy in fetch(turn):
            copy.wait()
        right = jnp.concatenate(
            [
                jnp.concatenate(
                    [
                        kept(
                            up_on[i, turn * each + c],
                            up_buf[slot, i * block : (i + 1) * block, c * block : (c + 1) * block],
                        )
                        for c in range(each)
                    ],
                    1,
                )
                for i in range(down)
            ],
            0,
        )
        pre = jnp.dot(full[0], right, preferred_element_type=jnp.float32)
        sums[0, :, lanes] = pre.astype(jnp.bfloat16)
        right = jnp.concatenate(
            [
                jnp.concatenate(
                    [
                        kept(
                            down_on[turn * each + c, i],
                            down_buf[
                                slot, c * block : (c + 1) * block, i * block : (i + 1) * block
                            ],
                        )
                        for i in range(down)
                    ],
                    1,
                )
                for c in range(each)
            ],
            0,
        )
        dact = lax.dot_general(
            full[1], right, (((1,), (1,)), ((), ())), preferred_element_type=jnp.float32
        )
        sums[1, :, lanes] = dact.astype(jnp.bfloat16)

        @pl.when(turn + slots < turns)
        def _():
            for copy in fetch(turn + slots):
                copy.start()

        for copy in leave(turn):
            copy.start()
        return carry

    lax.fori_loop(0, turns, step, 0)
    for turn in range(turns):
        for copy in leave(turn):
            copy.wait()
    whole.wait()


def forward(held, orders, height, up_weight, down_weight, up_on, down_on, after):
    width, hidden = up_weight.shape
    block = width // up_on.shape[0]
    rows = 2 * held[0][0].shape[1]
    moves, arrays, lane = [], [], 0
    for (low, high), order in zip(held, orders):
        for side, source, target, tall in runs(order, height, rows // 2):
            moves.append((len(arrays) + side, source, target, tall, lane, low.shape[2]))
        arrays += [low, high]
        lane += low.shape[2]
    any_space = pl.BlockSpec(memory_space=pl.ANY)
    smem = pl.BlockSpec(memory_space=pltpu.SMEM)
    each = divisor(hidden // block, 2)
    slots = 3
    shapes = [
        ((2, rows, width), jnp.bfloat16),
        ((2, rows, hidden), jnp.bfloat16),
    ]
    return pl.pallas_call(
        functools.partial(forward_kernel, moves, block),
        in_specs=[smem] * 2 + [any_space] * (len(arrays) + 2 + len(after)),
        out_specs=[any_space] * 3,
        scratch_shapes=[pltpu.VMEM(*shape) for shape in shapes]
        + [
            pltpu.VMEM((slots, width, each * block), jnp.bfloat16),
            pltpu.VMEM((slots, each * block, width), jnp.bfloat16),
            pltpu.SemaphoreType.DMA((len(moves),)),
            pltpu.SemaphoreType.DMA((2, hidden // block // each)),
            pltpu.SemaphoreType.DMA((2, slots)),
            pltpu.SemaphoreType.DMA,
        ],
        out_shape=[jax.ShapeDtypeStruct(*shape) for shape in shapes[:1]]
        + [jax.ShapeDtypeStruct((rows, hidden), jnp.bfloat16)] * 2,
        compiler_params=pltpu.CompilerParams(vmem_limit_bytes=48 * 1024 * 1024),
        cost_estimate=pl.CostEstimate(
            flops=rows * width, bytes_accessed=rows * width, transcendentals=0
        ),
        name="forward",
    )(up_on, down_on, *arrays, up_weight, down_weight, *after)


def backward_kernel(parts, block, up_on, dhid_ref, up_hbm, *refs):
    outs, (buf, sems) = refs[-2 - 2 * len(parts) : -2], refs[-2:]
    across = up_hbm.shape[1] // block
    tiles, at = [], 0
    for part, (moves, count) in enumerate(parts):
        each = divisor(count, 6)
        tiles += [(part, moves, at + r, r, each) for r in range(0, count, each)]
        at += count
    copies = []
    for k, (part, moves, row, lane, each) in enumerate(tiles):
        rows = pl.ds(row * block, each * block)
        copies.append(pltpu.make_async_copy(up_hbm.at[rows, :], buf.at[rows, :], sems.at[k]))
    for copy in copies:
        copy.start()
    for copy, (part, moves, row, lane, each) in zip(copies, tiles):
        copy.wait()
        right = jnp.concatenate(
            [
                jnp.concatenate(
                    [
                        kept(
                            up_on[row + r, c],
                            buf[(row + r) * block : (row + r + 1) * block, c * block : (c + 1) * block],
                        )
                        for c in range(across)
                    ],
                    1,
                )
                for r in range(each)
            ],
            0,
        )
        acc = lax.dot_general(
            dhid_ref[...], right, (((1,), (1,)), ((), ())), preferred_element_type=jnp.float32
        ).astype(jnp.bfloat16)
        for side, target, source, tall in moves:
            outs[2 * part + side][
                target : target + tall, lane * block : (lane + each) * block
            ] = acc[source : source + tall]


def backward(dhid, up_weight, up_on, orders, height, bounds, after):
    width, hidden = up_weight.shape
    block = width // up_on.shape[0]
    rows = dhid.shape[0]
    parts = [
        (runs(order, height, rows // 2), (stop - start) // block)
        for order, (start, stop) in zip(orders, bounds)
    ]
    tiles = sum(count // divisor(count, 6) for moves, count in parts)
    vmem = pl.BlockSpec(memory_space=pltpu.VMEM)
    smem = pl.BlockSpec(memory_space=pltpu.SMEM)
    any_space = pl.BlockSpec(memory_space=pl.ANY)
    outs = pl.pallas_call(
        functools.partial(backward_kernel, parts, block),
        in_specs=[smem, vmem] + [any_space] * (1 + len(after)),
        out_specs=[vmem] * (2 * len(parts)),
        scratch_shapes=[pltpu.VMEM((width, hidden), jnp.bfloat16), pltpu.SemaphoreType.DMA((tiles,))],
        out_shape=[
            jax.ShapeDtypeStruct((rows // 2, count * block), jnp.bfloat16)
            for moves, count in parts
            for side in range(2)
        ],
        compiler_params=pltpu.CompilerParams(vmem_limit_bytes=48 * 1024 * 1024),
        cost_estimate=pl.CostEstimate(
            flops=rows * width, bytes_accessed=rows * width, transcendentals=0
        ),
        name="backward",
    )(up_on, dhid, up_weight, *after)
    return [(outs[2 * part], outs[2 * part + 1]) for part in range(len(parts))]


def grad_kernel(block, factor, first, groups, pattern, *refs):
    lefts, rights, out_ref = refs[:groups], refs[groups : 2 * groups], refs[-1]
    down, across = out_ref.shape[0] // block, out_ref.shape[1] // block
    row = first[0] + pl.program_id(0) * down
    column = first[1] + pl.program_id(1) * across
    chunk = 2 if across % 2 == 0 else 1
    left = jnp.concatenate([ref[...] for ref in lefts], axis=0)
    for c in range(0, across, chunk):
        lanes = slice(c * block, (c + chunk) * block)
        acc = lax.dot_general(
            left,
            jnp.concatenate([ref[:, lanes] for ref in rights], axis=0),
            (((0,), (0,)), ((), ())),
            preferred_element_type=jnp.float32,
        )
        for r in range(down):
            for q in range(chunk):
                scale = jnp.where(pattern[row + r, column + c + q] != 0, factor, 0.0)
                out_ref[r * block : (r + 1) * block, (c + q) * block : (c + q + 1) * block] = (
                    acc[r * block : (r + 1) * block, q * block : (q + 1) * block] * scale
                ).astype(jnp.bfloat16)


def grad(lefts, rights, pattern, block, most, left_which, right_which, shares, by_column):
    groups = len(lefts)
    tall, broad = lefts[0].shape[-1], rights[0].shape[-1]
    tile = (
        divisor(tall // block // (1 if by_column else shares), most[0]) * block,
        divisor(broad // block // (shares if by_column else 1), most[1]) * block,
    )
    rows = lefts[0].shape[-2]
    tokens = groups * rows
    factor = float(1.0 / tokens**0.5)
    steps = [tall // tile[0], broad // tile[1]]
    steps[int(by_column)] //= shares

    def spec(which, breadth, index):
        if which is None:
            return pl.BlockSpec((rows, breadth), lambda i, c, *_: (0, index(i, c)))
        return pl.BlockSpec((None, rows, breadth), lambda i, c, *_: (which, 0, index(i, c)))

    def make(share):
        off = (0, share * steps[1]) if by_column else (share * steps[0], 0)

        def call(out, after):
            in_specs = [spec(left_which, tile[0], lambda i, c: off[0] + i)] * groups
            in_specs += [spec(right_which, tile[1], lambda i, c: off[1] + c)] * groups
            args = [*lefts, *rights, *after]
            in_specs += [pl.BlockSpec(memory_space=pl.ANY)] * len(after)
            aliases = {}
            if out is not None:
                in_specs.append(pl.BlockSpec(memory_space=pl.ANY))
                args.append(out)
                aliases = {len(args): 0}
            return pl.pallas_call(
                functools.partial(
                    grad_kernel,
                    block,
                    factor,
                    (off[0] * tile[0] // block, off[1] * tile[1] // block),
                    groups,
                ),
                grid_spec=pltpu.PrefetchScalarGridSpec(
                    num_scalar_prefetch=1,
                    grid=tuple(steps),
                    in_specs=in_specs,
                    out_specs=pl.BlockSpec(tile, lambda i, c, *_: (off[0] + i, off[1] + c)),
                ),
                out_shape=jax.ShapeDtypeStruct((tall, broad), jnp.bfloat16),
                input_output_aliases=aliases,
                compiler_params=pltpu.CompilerParams(vmem_limit_bytes=48 * 1024 * 1024),
                cost_estimate=pl.CostEstimate(
                    flops=tall * broad // shares,
                    bytes_accessed=tokens * broad // shares,
                    transcendentals=0,
                ),
                name="grad",
            )(pattern, *args)

        return call

    return [make(share) for share in range(shares)]


def add(left, right):
    return (left.astype(jnp.float32) + right.astype(jnp.float32)).astype(jnp.bfloat16)


def halves(value):
    half = value.shape[0] // 2
    return (value[:half], value[half:])


def on_device(sizes, tokens, up_weight, down_weight, cotangent, up_pattern, down_pattern):
    n, across = sizes["col"], sizes["row"]
    bits = n.bit_length() - 1
    far = list(range(bits - 1, 1, -1))
    outer, near = far[:-1], far[-1:]
    orders = [[*outer, 1, *near, 0], [*outer, *near, 0, 1], [*outer, 0, 1, *near]]
    width, hidden = up_weight.shape
    down = up_pattern.shape[0]
    block = width // down
    height = tokens.shape[0] // GROUPS
    bounds = [0, SPLIT[0] * down // OUT_OF, sum(SPLIT) * down // OUT_OF, down]
    bounds = [(at * block, to * block) for at, to in zip(bounds, bounds[1:])]

    def swap(value, bit):
        return lax.ppermute(value, "col", [(i, i ^ (1 << bit)) for i in range(n)])

    def later(value, *marks):
        return lax.optimization_barrier((value, *marks))[0]

    def beside(sums, marks):
        for bit in range(across.bit_length() - 1):
            pairs = [(i, i ^ (1 << bit)) for i in range(across)]
            others = [later(lax.ppermute(part.astype(jnp.bfloat16), "row", pairs), *marks) for part in sums]
            sums = [
                part.astype(jnp.float32) + other.astype(jnp.float32) for part, other in zip(sums, others)
            ]
        return sums

    helds = []
    for g in range(GROUPS):
        rows = slice(g * height, (g + 1) * height)
        own = jnp.stack([tokens[rows], cotangent[rows]])
        if g > 0:
            own = later(own, *ahead)
        for bit in outer:
            own = jnp.concatenate([own, swap(own, bit)], axis=1)
        if g > 0:
            own = later(own, *helds[-1])
        held, ahead = [], []
        for part, (start, stop) in enumerate(bounds):
            low = own[:, :, start:stop]
            rest = orders[part][len(outer) :]
            for bit in rest[:-1]:
                low = jnp.concatenate([low, swap(low, bit)], axis=1)
                if bit == rest[0]:
                    ahead.append(low)
            held.append(low)
        helds.append(held)
    for g, held in enumerate(helds):
        marks = helds[g + 1] if g + 1 < GROUPS else []
        helds[g] = [(low, swap(later(low, *marks), order[-1])) for low, order in zip(held, orders)]

    def stage(held, at, mark, marked):
        summed = []
        for part, (low, high) in enumerate(held):
            other = swap(high, orders[part][-1 - at])
            summed.append(add(low, other if mark is None or part >= marked else later(other, mark)))
        return summed

    def finish(summed, mark):
        total = jnp.concatenate(summed, axis=1)
        for bit in reversed(outer):
            low, high = halves(total)
            other = swap(high, bit)
            total = add(low, other if mark is None else later(other, mark))
        return total

    stages = len(orders[0]) - len(outer)
    last = GROUPS - 1
    fulls, actives, dhids, totals = [], [], [], []
    for g in range(GROUPS):
        after = [low for low, high in helds[g + 1]] if g + 1 < GROUPS else []
        after = after + ([half for pair in totals[-1] for half in pair] if g > 0 else [])
        full, *sums = forward(
            helds[g], orders, height, up_weight, down_weight, up_pattern, down_pattern, after
        )
        marks = [high for low, high in helds[g + 1][:2]] if g + 1 < GROUPS else []
        active, dhid = activate(*beside(sums, marks))
        fulls.append(full)
        actives.append(active)
        dhids.append(dhid)
        early, after = totals, []
        if g == last:
            for at, mark in zip(range(stages - 1), (sums[1], dhid)):
                early = [stage(held, at, mark, len(orders)) for held in early]
                after = [total for summed in early for total in summed]
                early = [[halves(total) for total in summed] for summed in early]
        totals.append(
            backward(dhid, up_weight, up_pattern, orders, height, bounds, after)
        )

    grads = [
        grad(fulls, dhids, up_pattern, block, (8, 12), 0, None, 2, False),
        grad(actives, fulls, down_pattern, block, (12, 8), None, 1, 2, True),
    ]
    work = [(which, call) for pair in zip(*grads) for which, call in enumerate(pair)]
    outs = [None, None]

    def advance(count, after):
        for which, call in work[:count]:
            outs[which] = call(outs[which], after)
        del work[:count]

    held = totals[last]
    advance(2, [half for pair in held for half in pair])
    late = [stage(pairs, stages - 1, outs[1], len(orders)) for pairs in early]
    for at in range(stages):
        summed = stage(held, at, outs[1 - at] if at < 2 else None, 2)
        if at == 0:
            advance(1, summed)
            shares = [finish(done, outs[0]) for done in late]
        if at < stages - 1:
            summed = lax.optimization_barrier(summed)
        held = [halves(total) for total in summed]
    advance(len(work), summed)
    shares.append(finish(summed, None))
    input_grad = jnp.concatenate(shares, axis=0)
    return (input_grad, outs[0], outs[1])


def solution(mesh):
    return jax.shard_map(
        functools.partial(on_device, dict(mesh.shape)),
        mesh=mesh,
        in_specs=(
            P("col", "row"),
            P("row", "col"),
            P("col", "row"),
            P("col", "row"),
            P("row", "col"),
            P("col", "row"),
        ),
        out_specs=(P("col", "row"), P("row", "col"), P("col", "row")),
        check_vma=False,
    )
```
